32 devices in a mesh: re: 16 (over z, y, core), kq: 2 (over x).
Axes of the slice: x: 2, y: 2, z: 4, core: 2. Of those that a mesh axis runs over, the one named last changes fastest.
Arguments:
- couplings: bfloat16 [2, 64, 2, 18, 1024], P(None, 're'), may hold values from -0.41992188 to 0.41992188
- re_vectors: int32 [64, 3], P('re'), may hold values from -8 to 8
- degeneracy: int32 [64], P('re'), may hold values from 1 to 8
- kpoints: int32 [64, 3], P('kq'), may hold values from 0 to 15
- plus_index: int32 [64, 2], P('kq'), may hold values from 0 to 63, as said below
- mode_vectors: float32 [2, 2, 18, 18], replicated, may hold values from -1 to 1
- band_vectors: float32 [64, 2, 32, 16], P('kq'), may hold values from -0.75 to 0.75
Outputs:
- rotated_couplings: float32 [2, 16, 72, 512], P('kq', 're')
The draws below stay inside these ranges and needn't reach their ends.
Inputs may be any that keep to these rules, and one draw needn't show every extreme that they name: `plus_index`: each column lists every one of the 64 fine k points exactly once.
All inputs are finite; a program needn't handle non-finite values.
Results may differ from the reference program's by a relative error of at most 0.0023.
Values may be sent and summed in bfloat16 or wider, within the bound.
A program may use at most 128 MiB of HBM per device.

```python
import math
import jax
import jax.numpy as jnp
from jax import lax

W = 32
NB = 16
M = 18
Q = 2
NG = 16
RMAX = 8
K = 64
RE = 64
ROWS_DEV = 72
N_RE = 16
N_KQ = 2


def draw_plus_index(key, part):
    columns = [jax.random.permutation(jax.random.fold_in(key, 11 + column_id), K) for column_id in range(Q)]
    return jnp.stack(columns, axis=1).astype(jnp.int32)


def set_ends(entries, key, least, top_value):
    shape = entries.shape
    place = [jax.random.randint(jax.random.fold_in(key, axis), (), 0, shape[axis]) for axis in range(len(shape))]
    entries = entries.at[tuple(place)].set(least)
    longest = shape.index(max(shape))
    place[longest] = (place[longest] + 1) % shape[longest]
    return entries.at[tuple(place)].set(top_value)


def block_scale(own_key, shape, pieces, least, largest):
    def one(position, blocks):
        draws = jax.random.uniform(jax.random.fold_in(jax.random.fold_in(own_key, 6), position), (blocks,), jnp.float32, least / len(pieces), largest / len(pieces))
        return jnp.repeat(jnp.exp(draws), shape[position] // blocks).reshape((-1,) + (1,) * (len(shape) - position - 1))

    loudness = one(*pieces[0])
    for cut in pieces[1:]:
        loudness = loudness * one(*cut)
    return loudness


def scatter_about(own_key, extent, width, limit, cuts=(), held_as=jnp.bfloat16):
    loudness = block_scale(own_key, extent, cuts, -0.22, 0.18) if cuts else 1.0
    array = jax.random.normal(own_key, extent, jnp.float32) * width * loudness
    return jnp.minimum(jnp.maximum(array, -limit), limit).astype(held_as)


def setup_inputs(seed: int = 0) -> dict:
    splits = jax.random.split(jax.random.key(seed), 8)
    return {
        "couplings": scatter_about(splits[0], (2, RE, Q, M, W * W), 0.07, 0.41992188, ((1, 16),)),
        "re_vectors": set_ends(jax.random.randint(splits[1], (RE, 3), 0 - RMAX, RMAX + 1), jax.random.fold_in(splits[1], 1), 0 - RMAX, RMAX).astype(jnp.int32),
        "degeneracy": set_ends(jax.random.randint(splits[2], (RE,), 1, 9), jax.random.fold_in(splits[2], 1), 1, 8).astype(jnp.int32),
        "kpoints": set_ends(jax.random.randint(splits[3], (K, 3), 0, NG), jax.random.fold_in(splits[3], 1), 0, NG - 1).astype(jnp.int32),
        "plus_index": draw_plus_index(jax.random.fold_in(splits[7], 71), 0),
        "mode_vectors": scatter_about(splits[5], (Q, 2, M, M), 0.167, 1.0, (), jnp.float32),
        "band_vectors": scatter_about(splits[6], (K, 2, W, NB), 0.125, 0.75, ((0, 2),), jnp.float32),
    }


precise = lax.Precision.HIGHEST


def phase_matrix(kint, rint, degen):
    product = jnp.sum(kint[:, None, :] * rint[None, :, :], axis=-1)
    angle = jnp.mod(product, NG).astype(jnp.float32) * (2.0 * math.pi / NG)
    weight = 1.0 / degen.astype(jnp.float32)
    cosine = jnp.cos(angle) * weight[None, :]
    sine = jnp.sin(angle) * weight[None, :]
    upper = jnp.concatenate([cosine, -sine], axis=1)
    lower = jnp.concatenate([sine, cosine], axis=1)
    return jnp.concatenate([upper, lower], axis=0).astype(jnp.bfloat16)


def rotate_modes(real_part, imag_part, vectors):
    er = vectors[:, 0]
    ei = vectors[:, 1]
    out_real = jnp.einsum('qvu,kqvx->kqux', er, real_part, precision=precise) - jnp.einsum('qvu,kqvx->kqux', ei, imag_part, precision=precise)
    out_imag = jnp.einsum('qvu,kqvx->kqux', er, imag_part, precision=precise) + jnp.einsum('qvu,kqvx->kqux', ei, real_part, precision=precise)
    return out_real, out_imag


def project_right(real_part, imag_part, factor):
    fr = factor[:, 0]
    fi = factor[:, 1]
    out_real = jnp.einsum('rmn,rnj->rmj', real_part, fr, precision=precise) - jnp.einsum('rmn,rnj->rmj', imag_part, fi, precision=precise)
    out_imag = jnp.einsum('rmn,rnj->rmj', real_part, fi, precision=precise) + jnp.einsum('rmn,rnj->rmj', imag_part, fr, precision=precise)
    return jnp.stack([out_real, out_imag], axis=1)


def project_left(values, factor):
    fr = factor[:, 0]
    fi = factor[:, 1]
    xr = values[:, 0]
    xi = values[:, 1]
    out_real = jnp.einsum('rmi,rmj->rij', fr, xr, precision=precise) + jnp.einsum('rmi,rmj->rij', fi, xi, precision=precise)
    out_imag = jnp.einsum('rmi,rmj->rij', fr, xi, precision=precise) - jnp.einsum('rmi,rmj->rij', fi, xr, precision=precise)
    return jnp.stack([out_real, out_imag], axis=1)


def reference(couplings, re_vectors, degeneracy, kpoints, plus_index, mode_vectors, band_vectors):
    phases = phase_matrix(kpoints, re_vectors, degeneracy).astype(jnp.float32)
    total_re = couplings.shape[1]
    stacked = couplings.astype(jnp.float32).reshape(2 * total_re, -1)
    bloch = jnp.dot(phases, stacked, precision=precise)
    total_k = kpoints.shape[0]
    bloch = bloch.reshape(2, total_k, Q, M, W * W)
    moded_real, moded_imag = rotate_modes(bloch[0], bloch[1], mode_vectors)
    row_count = total_k * Q * M
    row_ids = jnp.arange(row_count, dtype=jnp.int32)
    k_rows = row_ids // (Q * M)
    q_rows = (row_ids // M) % Q
    right = project_right(moded_real.reshape(row_count, W, W), moded_imag.reshape(row_count, W, W), band_vectors[k_rows])
    plus_rows = plus_index[k_rows, q_rows]
    result = project_left(right, band_vectors[plus_rows])
    return result.reshape(N_KQ, N_RE, ROWS_DEV, 2 * NB * NB)
```

```python
import functools
import math

import jax
import jax.numpy as jnp
from jax import lax
from jax.experimental import pallas as pl
from jax.experimental.pallas import tpu as pltpu
from jax.sharding import PartitionSpec as P

W = 32
NB = 16
M = 18
Q = 2
NG = 16


precise = lax.Precision.HIGHEST


def phase_matrix(kint, rint, degen):
    product = jnp.sum(kint[:, None, :] * rint[None, :, :], axis=-1)
    angle = jnp.mod(product, NG).astype(jnp.float32) * (2.0 * math.pi / NG)
    weight = 1.0 / degen.astype(jnp.float32)
    cosine = jnp.cos(angle) * weight[None, :]
    sine = jnp.sin(angle) * weight[None, :]
    upper = jnp.concatenate([cosine, -sine], axis=1)
    lower = jnp.concatenate([sine, cosine], axis=1)
    return jnp.concatenate([upper, lower], axis=0).astype(jnp.bfloat16)


def phase_sum(kint, rint, degen, values):
    phases = phase_matrix(kint, rint, degen)
    lattice_count = values.shape[1]
    stacked = values.reshape(2 * lattice_count, -1)
    bloch = jnp.dot(phases, stacked, preferred_element_type=jnp.float32)
    return bloch.reshape(2, kint.shape[0], Q, M, -1)


def rotate_modes(real_part, imag_part, vectors):
    er = vectors[:, 0]
    ei = vectors[:, 1]
    out_real = jnp.einsum("qvu,kqvx->kqux", er, real_part, precision=precise) - jnp.einsum(
        "qvu,kqvx->kqux", ei, imag_part, precision=precise
    )
    out_imag = jnp.einsum("qvu,kqvx->kqux", er, imag_part, precision=precise) + jnp.einsum(
        "qvu,kqvx->kqux", ei, real_part, precision=precise
    )
    return (out_real, out_imag)


def project_right(real_part, imag_part, factor):
    fr = factor[:, 0]
    fi = factor[:, 1]
    out_real = jnp.einsum("rmn,rnj->rmj", real_part, fr, precision=precise) - jnp.einsum(
        "rmn,rnj->rmj", imag_part, fi, precision=precise
    )
    out_imag = jnp.einsum("rmn,rnj->rmj", real_part, fi, precision=precise) + jnp.einsum(
        "rmn,rnj->rmj", imag_part, fr, precision=precise
    )
    return jnp.stack([out_real, out_imag], axis=1)


def project_left(values, factor):
    fr = factor[:, 0]
    fi = factor[:, 1]
    xr = values[:, 0]
    xi = values[:, 1]
    out_real = jnp.einsum("rmi,rmj->rij", fr, xr, precision=precise) + jnp.einsum(
        "rmi,rmj->rij", fi, xi, precision=precise
    )
    out_imag = jnp.einsum("rmi,rmj->rij", fr, xi, precision=precise) - jnp.einsum(
        "rmi,rmj->rij", fi, xr, precision=precise
    )
    return jnp.stack([out_real, out_imag], axis=1)


def plus_bands(plus_index, band_vectors, pair_ids):
    targets = plus_index[pair_ids // Q, pair_ids % Q]
    every_band = lax.all_gather(band_vectors, "kq", axis=0, tiled=True)
    return every_band[targets]


def shards(couplings, re_vectors, degeneracy, kpoints, plus_index, mode_vectors, band_vectors):
    local_count = kpoints.shape[0]
    local_rows = local_count * Q * M
    share_rows = local_rows // lax.axis_size("re")
    share_pairs = share_rows // M
    share_ids = lax.axis_index("re") * share_rows + jnp.arange(share_rows, dtype=jnp.int32)
    pair_share = lax.axis_index("re") * share_pairs + jnp.arange(share_pairs, dtype=jnp.int32)
    local_share = jnp.arange(share_rows, dtype=jnp.int32) // M
    moved = lax.all_to_all(couplings, "re", split_axis=4, concat_axis=1, tiled=True)
    lattice_all, degen_all = (
        lax.all_gather(re_vectors, "re", axis=0, tiled=True),
        lax.all_gather(degeneracy, "re", axis=0, tiled=True),
    )
    columns = moved.shape[4]
    bloch = phase_sum(kpoints, lattice_all, degen_all, moved)
    moded_real, moded_imag = rotate_modes(bloch[0], bloch[1], mode_vectors)
    paired = jnp.stack([moded_real, moded_imag]).reshape(2, local_rows, columns)
    returned = lax.all_to_all(paired, "re", split_axis=1, concat_axis=2, tiled=True)
    right = project_right(
        returned[0].reshape(share_rows, W, W),
        returned[1].reshape(share_rows, W, W),
        band_vectors[share_ids // (Q * M)],
    )
    fetched = plus_bands(plus_index, band_vectors, pair_share)
    result = project_left(right, fetched[local_share])
    return result.reshape(1, 1, share_rows, 2 * NB * NB)


MESH = pl.DeviceIdType.MESH
LANES = 640
GEO = 576
f32 = jnp.float32
bf16 = jnp.bfloat16
NT = (((1,), (1,)), ((), ()))
TN = (((0,), (0,)), ((), ()))


def iota(shape, axis):
    return lax.broadcasted_iota(jnp.int32, shape, axis)


def exact(a, b, dims=(((1,), (0,)), ((), ()))):
    return lax.dot_general(a, b, dims, precision=precise, preferred_element_type=f32)


def split(a):
    high = a.astype(bf16)
    return high, (a - high.astype(f32)).astype(bf16)


def dot16(a, b):
    return jnp.dot(a, b, preferred_element_type=f32)


def unit_cosine(step):
    step = step - NG * jnp.floor(step * (1.0 / NG))
    fold = jnp.minimum(step, NG - step)
    near = jnp.minimum(fold, 8.0 - fold)
    size = jnp.where(near < 0.5, 1.0, jnp.where(near < 1.5, math.cos(math.pi / 8), math.cos(math.pi / 4)))
    size = jnp.where(near > 2.5, math.cos(3 * math.pi / 8), size)
    size = jnp.where(near > 3.5, 0.0, size)
    return jnp.where(fold > 4.5, -size, size)


def quarter_swap(parts):
    lane = iota(parts[0].shape, 1)
    upper = (lane & 64) != 0
    odd = (lane & 32) != 0
    stage = list(parts)
    for a, b in ((0, 2), (1, 3)):
        moved = pltpu.roll(jnp.where(upper, parts[a], parts[b]), 64, 1)
        stage[a] = jnp.where(upper, moved, parts[a])
        stage[b] = jnp.where(upper, parts[b], moved)
    out = list(stage)
    for a, b in ((0, 1), (2, 3)):
        out[a] = jnp.where(odd, pltpu.roll(stage[b], 32, 1), stage[a])
        out[b] = jnp.where(odd, stage[b], pltpu.roll(stage[a], 96, 1))
    return out


def group_swap(x):
    sub = iota(x.shape, 0)
    group = iota(x.shape, 1) // 16
    rows = x.shape[0]
    for s in (4, 2, 1):
        low_a = (sub & s) == 0
        low_b = (group & s) == 0
        down = pltpu.roll(pltpu.roll(x, rows - s, 0), 16 * s, 1)
        up = pltpu.roll(pltpu.roll(x, s, 0), 128 - 16 * s, 1)
        x = jnp.where(low_a == low_b, x, jnp.where(low_a, down, up))
    return x


def unpack_bands(tile):
    return jnp.concatenate([tile] + [pltpu.roll(tile, 128 - 32 * g, 1) for g in (1, 2, 3)], axis=0)


def kernel(
    n_re, n_kq, coup, geo, kp, bz, mode, plus, out,
    F, Y, X, S, D, BZ, KP, send1, recv1, send2, recv2, sendb, recvb,
):
    re = lax.axis_index("re")
    kq = lax.axis_index("kq")
    n_all = n_re * n_kq
    me = kq * n_re + re
    barrier = pltpu.get_barrier_semaphore()

    def hello(off, carry):
        to = lax.rem(me + off, n_all)
        pl.semaphore_signal(
            barrier, inc=1, device_id=(lax.rem(to, n_re), to // n_re), device_id_type=MESH
        )
        return carry

    lax.fori_loop(1, n_all, hello, 0)

    width = n_re * W
    tiles = width // 128
    for a in range(16):
        c, r, q = a // 8, (a // 2) % 4, a % 2
        for t in range(tiles):
            lanes = pl.ds(pl.multiple_of(kq * width + t * 128, 128), 128)
            F[t, a * 24 : a * 24 + M, :] = coup[c, r, q, :, lanes].astype(f32)
    spare = geo[...]
    for t in range(tiles):
        for v4 in range(5):
            parts = []
            for v in range(4 * v4, 4 * v4 + 4):
                if v < M:
                    parts.append(F[t, pl.ds(v, 16, stride=24), :])
                else:
                    parts.append(jnp.zeros((16, 128), f32))
            moved = quarter_swap(parts)
            for m in range(4):
                piece = moved[m] + spare if v4 == 4 else moved[m]
                Y[t * 4 + m, :, v4 * 128 : v4 * 128 + 128] = piece.astype(bf16)

    pl.semaphore_wait(barrier, n_all - 1)

    def first(to, frm):
        return pltpu.make_async_remote_copy(
            src_ref=Y.at[to], dst_ref=X.at[frm],
            send_sem=send1.at[to], recv_sem=recv1.at[frm],
            device_id=(to, kq), device_id_type=MESH,
        )

    def swap(ref, full, s, off):
        other = lax.rem(kq + off, n_kq)
        return pltpu.make_async_remote_copy(
            src_ref=ref, dst_ref=full.at[kq],
            send_sem=sendb.at[s, other], recv_sem=recvb.at[s, kq],
            device_id=(re, other), device_id_type=MESH,
        )

    def swapped(ref, full, s, off):
        other = lax.rem(kq + off, n_kq)
        return pltpu.make_async_remote_copy(
            src_ref=ref, dst_ref=full.at[other],
            send_sem=sendb.at[s, other], recv_sem=recvb.at[s, other],
            device_id=(re, other), device_id_type=MESH,
        )

    for off in range(1, n_kq):
        swap(kp, KP, 0, off).start()

    def go1(off, carry):
        first(lax.rem(re + off, n_re), re).start()
        return carry

    lax.fori_loop(1, n_re, go1, 0)
    for off in range(1, n_kq):
        swap(bz, BZ, 1, off).start()
    X[re] = Y[re]
    KP[kq] = kp[...]
    BZ[kq] = bz[...]
    for off in range(1, n_kq):
        swapped(kp, KP, 0, off).wait_recv()
    n_k = n_kq * kp.shape[0]
    rows = n_k * 4
    pick = ((iota((rows, n_k), 0) // 4) == iota((rows, n_k), 1)).astype(bf16)
    grid = dot16(pick, KP[...].reshape(n_k, 128).astype(bf16)).astype(bf16)

    def got1(off, carry):
        first(re, lax.rem(re + off, n_re)).wait_recv()
        return carry

    lax.fori_loop(1, n_re, got1, 0)
    depth = n_re * 16
    lattice = X[:, :, 512:640].reshape(depth, 128)
    product = lax.dot_general(grid, lattice, NT, preferred_element_type=f32)
    ones = (iota((rows, 128), 1) == 67).astype(bf16)
    degen = lax.dot_general(ones, lattice, NT, preferred_element_type=f32)
    row = iota((rows, depth), 0)
    col = iota((rows, depth), 1)
    turn = (((col // 8) & 1) - (row & 1)).astype(f32) * 4.0
    same = ((row // 2) & 1) == (col & 1)
    phases = jnp.where(same, unit_cosine(product + turn) * (1.0 / degen), 0.0).astype(bf16)
    for t in range(5):
        lanes = slice(t * 128, t * 128 + 128)
        bloch = dot16(phases, X[:, :, lanes].reshape(depth, 128))
        S[:, :, lanes] = bloch.reshape(n_all, 8, 128).astype(bf16)

    def second(to, frm):
        return pltpu.make_async_remote_copy(
            src_ref=S.at[to], dst_ref=D.at[frm],
            send_sem=send2.at[to], recv_sem=recv2.at[frm],
            device_id=(lax.rem(to, n_re), to // n_re), device_id_type=MESH,
        )

    def go2(off, carry):
        second(lax.rem(me + off, n_all), me).start()
        return carry

    lax.fori_loop(1, n_all, go2, 0)
    D[me] = S[me]

    for off in range(1, n_kq):
        swapped(bz, BZ, 1, off).wait_recv()
    spread = (iota((128, 256), 0) == iota((128, 256), 1) // 8).astype(f32)
    lane = iota((NB, 256), 1)
    imag_in = (lane & 1) == 1
    left = []
    for p in range(4):
        target = plus[re * 2 + p // 2, p % 2]
        n_dev = kp.shape[0]
        tile = BZ[target // n_dev, lax.rem(target, n_dev)]
        wide = exact(unpack_bands(tile), spread)
        real, imag = wide[:NB], wide[NB:]
        mine = ((lane // 2) & 3) == p
        left.append(jnp.where(mine, jnp.where(imag_in, imag, real), 0.0))
        left.append(jnp.where(mine, jnp.where(imag_in, real, -imag), 0.0))
    left_high, left_low = split(jnp.concatenate(left, axis=0))
    left_both = jnp.concatenate([left_high, left_low], axis=0)
    down = ((iota((256, 128), 0) & 31) == iota((256, 128), 1)).astype(f32)
    lane = iota((32, 256), 1)
    across = iota((32, 256), 0) == (lane // 128) * NB + (lane & 15)
    flip = iota((32, 256), 0) == (1 - lane // 128) * NB + (lane & 15)
    minus = jnp.where(lane < 128, -1.0, 1.0)
    same_mode = iota((256, 256), 0) // 32 == (iota((256, 256), 1) // NB) % 8
    right = []
    for k in range(2):
        tall = exact(down, unpack_bands(bz[re * 2 + k]), NT)
        a = exact(tall, across.astype(f32))
        b = exact(tall, jnp.where(flip, minus, 0.0))
        right.append([split(jnp.where(same_mode, w, 0.0)) for w in (a, b)])

    def got2(off, carry):
        second(me, lax.rem(me + off, n_all)).wait_recv()
        return carry

    lax.fori_loop(1, n_all, got2, 0)
    data = D[...].astype(f32).reshape(n_all * 8, LANES).astype(bf16)
    both = dot16(left_both, data)
    summed = both[:128] + both[128:]
    groups = [
        summed[:, 0:256],
        summed[:, 256:512],
        jnp.concatenate([summed[:, 512:640], jnp.zeros((128, 128), f32)], axis=1),
    ]
    values = [[None, None], [None, None]]
    for k in range(2):
        total = None
        for c in range(2):
            x = jnp.concatenate(
                [g[((k * 2 + q) * 2 + c) * NB : ((k * 2 + q) * 2 + c + 1) * NB] for g in groups for q in range(2)],
                axis=0,
            )
            high, low = split(x)
            w_high, w_low = right[k][c]
            term = dot16(high, w_high) + dot16(low, w_high) + dot16(high, w_low)
            total = term if total is None else total + term
        for c in range(2):
            turned = group_swap(total[:, c * 128 : c * 128 + 128])
            for q in range(2):
                values[q][c] = (values[q][c] or []) + [
                    jnp.concatenate(
                        [
                            jnp.concatenate(
                                [turned[(g * 2 + q) * NB + h * 8 : (g * 2 + q) * NB + h * 8 + 8] for g in range(3)],
                                axis=0,
                            )
                            for h in range(2)
                        ],
                        axis=1,
                    )
                ]
    for q in range(2):
        xr = jnp.concatenate(values[q][0], axis=1)[:M]
        xi = jnp.concatenate(values[q][1], axis=1)[:M]
        er, ei = mode[q, 0], mode[q, 1]
        yr = exact(er, xr, TN) - exact(ei, xi, TN)
        yi = exact(er, xi, TN) + exact(ei, xr, TN)
        for k in range(2):
            at = (k * 2 + q) * M
            out[0, 0, at : at + M, 0:256] = yr[:, k * 256 : k * 256 + 256]
            out[0, 0, at : at + M, 256:512] = yi[:, k * 256 : k * 256 + 256]

    for off in range(1, n_kq):
        swap(kp, KP, 0, off).wait_send()
        swap(bz, BZ, 1, off).wait_send()

    def sent1(off, carry):
        first(lax.rem(re + off, n_re), re).wait_send()
        return carry

    lax.fori_loop(1, n_re, sent1, 0)

    def sent2(off, carry):
        second(lax.rem(me + off, n_all), me).wait_send()
        return carry

    lax.fori_loop(1, n_all, sent2, 0)


def fused(n_re, n_kq, couplings, re_vectors, degeneracy, kpoints, plus_index, mode_vectors, band_vectors):
    n_all = n_re * n_kq
    k_dev = kpoints.shape[0]
    lattice = jnp.concatenate([re_vectors, degeneracy[:, None]], axis=1).astype(f32)
    lattice = jnp.broadcast_to(lattice[None, :, None, :], (2, 4, 2, 4)).reshape(16, 4)
    geo = jnp.pad(lattice, ((0, 0), (64, 60)))
    kp = jnp.pad(kpoints.astype(f32), ((0, 0), (64, 61)))
    bz = band_vectors.transpose(0, 1, 3, 2).reshape(k_dev, 4, 8, W).transpose(0, 2, 1, 3).reshape(k_dev, 8, 128)
    vmem = pl.BlockSpec(memory_space=pltpu.VMEM)
    return pl.pallas_call(
        functools.partial(kernel, n_re, n_kq),
        out_shape=jax.ShapeDtypeStruct((1, 1, k_dev * Q * M // n_re, 2 * NB * NB), f32),
        in_specs=[vmem] * 5 + [pl.BlockSpec(memory_space=pltpu.SMEM)],
        out_specs=vmem,
        scratch_shapes=[
            pltpu.VMEM((n_re * W // 128, 16 * 24, 128), f32),
            pltpu.VMEM((n_re, 16, LANES), bf16),
            pltpu.VMEM((n_re, 16, LANES), bf16),
            pltpu.VMEM((n_all, 8, LANES), bf16),
            pltpu.VMEM((n_all, 8, LANES), bf16),
            pltpu.VMEM((n_kq, k_dev, 8, 128), f32),
            pltpu.VMEM((n_kq, k_dev, 128), f32),
            pltpu.SemaphoreType.DMA((n_re,)),
            pltpu.SemaphoreType.DMA((n_re,)),
            pltpu.SemaphoreType.DMA((n_all,)),
            pltpu.SemaphoreType.DMA((n_all,)),
            pltpu.SemaphoreType.DMA((2, n_kq)),
            pltpu.SemaphoreType.DMA((2, n_kq)),
        ],
        compiler_params=pltpu.CompilerParams(
            collective_id=0, has_side_effects=True, vmem_limit_bytes=48 * 1024 * 1024
        ),
    )(couplings, geo, kp, bz, mode_vectors, plus_index)


def solution(mesh):
    n_re, n_kq = mesh.shape["re"], mesh.shape["kq"]
    body = functools.partial(fused, n_re, n_kq) if (n_re, n_kq) == (NB, W // NB) else shards
    return jax.shard_map(
        body,
        mesh=mesh,
        in_specs=(
            P(None, "re", None, None, None),
            P("re", None),
            P("re"),
            P("kq", None),
            P("kq", None),
            P(),
            P("kq", None, None, None),
        ),
        out_specs=P("kq", "re", None, None),
        check_vma=False,
    )
```

```python
import functools
import math

import jax
import jax.numpy as jnp
from jax import lax
from jax.experimental import pallas as pl
from jax.experimental.pallas import tpu as pltpu
from jax.sharding import PartitionSpec as P

W = 32
NB = 16
M = 18
Q = 2
NG = 16


precise = lax.Precision.HIGHEST


def phase_matrix(kint, rint, degen):
    product = jnp.sum(kint[:, None, :] * rint[None, :, :], axis=-1)
    angle = jnp.mod(product, NG).astype(jnp.float32) * (2.0 * math.pi / NG)
    weight = 1.0 / degen.astype(jnp.float32)
    cosine = jnp.cos(angle) * weight[None, :]
    sine = jnp.sin(angle) * weight[None, :]
    upper = jnp.concatenate([cosine, -sine], axis=1)
    lower = jnp.concatenate([sine, cosine], axis=1)
    return jnp.concatenate([upper, lower], axis=0).astype(jnp.bfloat16)


def phase_sum(kint, rint, degen, values):
    phases = phase_matrix(kint, rint, degen)
    lattice_count = values.shape[1]
    stacked = values.reshape(2 * lattice_count, -1)
    bloch = jnp.dot(phases, stacked, preferred_element_type=jnp.float32)
    return bloch.reshape(2, kint.shape[0], Q, M, -1)


def rotate_modes(real_part, imag_part, vectors):
    er = vectors[:, 0]
    ei = vectors[:, 1]
    out_real = jnp.einsum("qvu,kqvx->kqux", er, real_part, precision=precise) - jnp.einsum(
        "qvu,kqvx->kqux", ei, imag_part, precision=precise
    )
    out_imag = jnp.einsum("qvu,kqvx->kqux", er, imag_part, precision=precise) + jnp.einsum(
        "qvu,kqvx->kqux", ei, real_part, precision=precise
    )
    return (out_real, out_imag)


def project_right(real_part, imag_part, factor):
    fr = factor[:, 0]
    fi = factor[:, 1]
    out_real = jnp.einsum("rmn,rnj->rmj", real_part, fr, precision=precise) - jnp.einsum(
        "rmn,rnj->rmj", imag_part, fi, precision=precise
    )
    out_imag = jnp.einsum("rmn,rnj->rmj", real_part, fi, precision=precise) + jnp.einsum(
        "rmn,rnj->rmj", imag_part, fr, precision=precise
    )
    return jnp.stack([out_real, out_imag], axis=1)


def project_left(values, factor):
    fr = factor[:, 0]
    fi = factor[:, 1]
    xr = values[:, 0]
    xi = values[:, 1]
    out_real = jnp.einsum("rmi,rmj->rij", fr, xr, precision=precise) + jnp.einsum(
        "rmi,rmj->rij", fi, xi, precision=precise
    )
    out_imag = jnp.einsum("rmi,rmj->rij", fr, xi, precision=precise) - jnp.einsum(
        "rmi,rmj->rij", fi, xr, precision=precise
    )
    return jnp.stack([out_real, out_imag], axis=1)


def plus_bands(plus_index, band_vectors, pair_ids):
    targets = plus_index[pair_ids // Q, pair_ids % Q]
    every_band = lax.all_gather(band_vectors, "kq", axis=0, tiled=True)
    return every_band[targets]


def shards(couplings, re_vectors, degeneracy, kpoints, plus_index, mode_vectors, band_vectors):
    local_count = kpoints.shape[0]
    local_rows = local_count * Q * M
    share_rows = local_rows // lax.axis_size("re")
    share_pairs = share_rows // M
    share_ids = lax.axis_index("re") * share_rows + jnp.arange(share_rows, dtype=jnp.int32)
    pair_share = lax.axis_index("re") * share_pairs + jnp.arange(share_pairs, dtype=jnp.int32)
    local_share = jnp.arange(share_rows, dtype=jnp.int32) // M
    moved = lax.all_to_all(couplings, "re", split_axis=4, concat_axis=1, tiled=True)
    lattice_all, degen_all = (
        lax.all_gather(re_vectors, "re", axis=0, tiled=True),
        lax.all_gather(degeneracy, "re", axis=0, tiled=True),
    )
    columns = moved.shape[4]
    bloch = phase_sum(kpoints, lattice_all, degen_all, moved)
    moded_real, moded_imag = rotate_modes(bloch[0], bloch[1], mode_vectors)
    paired = jnp.stack([moded_real, moded_imag]).reshape(2, local_rows, columns)
    returned = lax.all_to_all(paired, "re", split_axis=1, concat_axis=2, tiled=True)
    right = project_right(
        returned[0].reshape(share_rows, W, W),
        returned[1].reshape(share_rows, W, W),
        band_vectors[share_ids // (Q * M)],
    )
    fetched = plus_bands(plus_index, band_vectors, pair_share)
    result = project_left(right, fetched[local_share])
    return result.reshape(1, 1, share_rows, 2 * NB * NB)


MESH = pl.DeviceIdType.MESH
LANES = 640
GEO = 576
f32 = jnp.float32
bf16 = jnp.bfloat16
NT = (((1,), (1,)), ((), ()))
TN = (((0,), (0,)), ((), ()))


def iota(shape, axis):
    return lax.broadcasted_iota(jnp.int32, shape, axis)


def exact(a, b, dims=(((1,), (0,)), ((), ()))):
    return lax.dot_general(a, b, dims, precision=precise, preferred_element_type=f32)


def split(a):
    high = a.astype(bf16)
    return high, (a - high.astype(f32)).astype(bf16)


def dot16(a, b):
    return jnp.dot(a, b, preferred_element_type=f32)


def unit_cosine(step):
    step = step - NG * jnp.floor(step * (1.0 / NG))
    fold = jnp.minimum(step, NG - step)
    near = jnp.minimum(fold, 8.0 - fold)
    size = jnp.where(near < 0.5, 1.0, jnp.where(near < 1.5, math.cos(math.pi / 8), math.cos(math.pi / 4)))
    size = jnp.where(near > 2.5, math.cos(3 * math.pi / 8), size)
    size = jnp.where(near > 3.5, 0.0, size)
    return jnp.where(fold > 4.5, -size, size)


def quarter_swap(parts):
    lane = iota(parts[0].shape, 1)
    upper = (lane & 64) != 0
    odd = (lane & 32) != 0
    stage = list(parts)
    for a, b in ((0, 2), (1, 3)):
        moved = pltpu.roll(jnp.where(upper, parts[a], parts[b]), 64, 1)
        stage[a] = jnp.where(upper, moved, parts[a])
        stage[b] = jnp.where(upper, parts[b], moved)
    out = list(stage)
    for a, b in ((0, 1), (2, 3)):
        out[a] = jnp.where(odd, pltpu.roll(stage[b], 32, 1), stage[a])
        out[b] = jnp.where(odd, stage[b], pltpu.roll(stage[a], 96, 1))
    return out


def group_swap(x):
    sub = iota(x.shape, 0)
    group = iota(x.shape, 1) // 16
    rows = x.shape[0]
    for s in (4, 2, 1):
        low_a = (sub & s) == 0
        low_b = (group & s) == 0
        down = pltpu.roll(pltpu.roll(x, rows - s, 0), 16 * s, 1)
        up = pltpu.roll(pltpu.roll(x, s, 0), 128 - 16 * s, 1)
        x = jnp.where(low_a == low_b, x, jnp.where(low_a, down, up))
    return x


def unpack_bands(tile):
    return jnp.concatenate([tile] + [pltpu.roll(tile, 128 - 32 * g, 1) for g in (1, 2, 3)], axis=0)


def kernel(
    n_re, n_kq, coup_any, rvec_any, degen_any, kp_any, plus_any, mode_any, bands_any, out,
    coup, rvec, degen_own, kp_own, plus, mode, bands,
    F, Y, X, S, D, BZ, KP, bz, kp, fetch, send1, recv1, send2, recv2, sendb, recvb,
):
    re = lax.axis_index("re")
    kq = lax.axis_index("kq")
    n_all = n_re * n_kq
    me = kq * n_re + re
    width = n_re * W
    tiles = width // 128
    mine = pl.ds(pl.multiple_of(kq * width, width), width)
    pairs = [
        (coup_any.at[:, :, :, :, mine], coup),
        (rvec_any, rvec),
        (degen_any, degen_own),
        (kp_any, kp_own),
        (bands_any, bands),
        (plus_any, plus),
        (mode_any, mode),
    ]
    loads = [pltpu.make_async_copy(a, b, fetch.at[n]) for n, (a, b) in enumerate(pairs)]
    for load in loads:
        load.start()
    barrier = pltpu.get_barrier_semaphore()

    def hello(off, carry):
        to = lax.rem(me + off, n_all)
        pl.semaphore_signal(
            barrier, inc=1, device_id=(lax.rem(to, n_re), to // n_re), device_id_type=MESH
        )
        return carry

    lax.fori_loop(1, n_all, hello, 0)

    for n in range(4):
        loads[n].wait()
    kp[...] = jnp.zeros_like(kp)
    kp[0:3, 0 : kp_own.shape[1]] = kp_own[...].astype(f32)
    row = iota((16, 128), 0) // 2 % 4
    lane = iota((16, 128), 1)
    spare = jnp.zeros((16, 128), f32)
    for r in range(4):
        for d in range(4):
            value = (rvec[r, d] if d < 3 else degen_own[r]).astype(f32)
            spare = jnp.where((row == r) & (lane == 64 + d), value, spare)
    for t in range(tiles):
        for a in range(8):
            F[t, :, 2 * a : 2 * a + 2, :] = coup[a // 4, a % 4, :, :, t * 128 : t * 128 + 128].astype(f32)
        for v4 in range(5):
            parts = []
            for v in range(4 * v4, 4 * v4 + 4):
                parts.append(F[t, v] if v < M else jnp.zeros((16, 128), f32))
            moved = quarter_swap(parts)
            for m in range(4):
                piece = moved[m] + spare if v4 == 4 else moved[m]
                Y[t * 4 + m, :, v4 * 128 : v4 * 128 + 128] = piece.astype(bf16)

    pl.semaphore_wait(barrier, n_all - 1)

    def first(to, frm):
        return pltpu.make_async_remote_copy(
            src_ref=Y.at[to], dst_ref=X.at[frm],
            send_sem=send1.at[to], recv_sem=recv1.at[frm],
            device_id=(to, kq), device_id_type=MESH,
        )

    def swap(ref, full, s, off):
        other = lax.rem(kq + off, n_kq)
        return pltpu.make_async_remote_copy(
            src_ref=ref, dst_ref=full.at[kq],
            send_sem=sendb.at[s, other], recv_sem=recvb.at[s, kq],
            device_id=(re, other), device_id_type=MESH,
        )

    def swapped(ref, full, s, off):
        other = lax.rem(kq + off, n_kq)
        return pltpu.make_async_remote_copy(
            src_ref=ref, dst_ref=full.at[other],
            send_sem=sendb.at[s, other], recv_sem=recvb.at[s, other],
            device_id=(re, other), device_id_type=MESH,
        )

    for off in range(1, n_kq):
        swap(kp, KP, 0, off).start()

    def go1(off, carry):
        first(lax.rem(re + off, n_re), re).start()
        return carry

    lax.fori_loop(1, n_re, go1, 0)
    loads[4].wait()
    for g in range(4):
        bz[:, :, g * 32 : g * 32 + 32] = bands[:, g // 2, g % 2 * 8 : g % 2 * 8 + 8, :]
    for off in range(1, n_kq):
        swap(bz, BZ, 1, off).start()
    loads[5].wait()
    loads[6].wait()
    X[re] = Y[re]
    KP[kq] = kp[...]
    BZ[kq] = bz[...]
    for off in range(1, n_kq):
        swapped(kp, KP, 0, off).wait_recv()
    n_dev = bz.shape[0]
    rows = n_kq * n_dev * 4
    points = KP[0]
    for other in range(1, n_kq):
        points = points + pltpu.roll(KP[other], other * n_dev, 1)
    points = jnp.concatenate([jnp.zeros((64, 128), f32), points, jnp.zeros((56, 128), f32)], axis=0)
    pick = ((iota((rows, 128), 0) // 4) == iota((rows, 128), 1)).astype(bf16)
    grid = lax.dot_general(pick, points.astype(bf16), NT, preferred_element_type=f32).astype(bf16)

    def got1(off, carry):
        first(re, lax.rem(re + off, n_re)).wait_recv()
        return carry

    lax.fori_loop(1, n_re, got1, 0)
    depth = n_re * 16
    lattice = X[:, :, 512:640].reshape(depth, 128)
    product = lax.dot_general(grid, lattice, NT, preferred_element_type=f32)
    ones = (iota((rows, 128), 1) == 67).astype(bf16)
    degen = lax.dot_general(ones, lattice, NT, preferred_element_type=f32)
    row = iota((rows, depth), 0)
    col = iota((rows, depth), 1)
    turn = (((col // 8) & 1) - (row & 1)).astype(f32) * 4.0
    same = ((row // 2) & 1) == (col & 1)
    phases = jnp.where(same, unit_cosine(product + turn) * (1.0 / degen), 0.0).astype(bf16)
    for t in range(5):
        lanes = slice(t * 128, t * 128 + 128)
        bloch = dot16(phases, X[:, :, lanes].reshape(depth, 128))
        S[:, :, lanes] = bloch.reshape(n_all, 8, 128).astype(bf16)

    def second(to, frm):
        return pltpu.make_async_remote_copy(
            src_ref=S.at[to], dst_ref=D.at[frm],
            send_sem=send2.at[to], recv_sem=recv2.at[frm],
            device_id=(lax.rem(to, n_re), to // n_re), device_id_type=MESH,
        )

    def go2(off, carry):
        second(lax.rem(me + off, n_all), me).start()
        return carry

    lax.fori_loop(1, n_all, go2, 0)
    D[me] = S[me]

    for off in range(1, n_kq):
        swapped(bz, BZ, 1, off).wait_recv()
    spread = (iota((128, 256), 0) == iota((128, 256), 1) // 8).astype(f32)
    lane = iota((NB, 256), 1)
    imag_in = (lane & 1) == 1
    left = []
    for p in range(4):
        target = plus[p % 2, re * 2 + p // 2]
        tile = BZ[target // n_dev, lax.rem(target, n_dev)]
        wide = exact(unpack_bands(tile), spread)
        real, imag = wide[:NB], wide[NB:]
        own = ((lane // 2) & 3) == p
        left.append(jnp.where(own, jnp.where(imag_in, imag, real), 0.0))
        left.append(jnp.where(own, jnp.where(imag_in, real, -imag), 0.0))
    left_high, left_low = split(jnp.concatenate(left, axis=0))
    left_both = jnp.concatenate([left_high, left_low], axis=0)
    down = ((iota((256, 128), 0) & 31) == iota((256, 128), 1)).astype(f32)
    lane = iota((32, 256), 1)
    across = iota((32, 256), 0) == (lane // 128) * NB + (lane & 15)
    flip = iota((32, 256), 0) == (1 - lane // 128) * NB + (lane & 15)
    minus = jnp.where(lane < 128, -1.0, 1.0)
    same_mode = iota((256, 256), 0) // 32 == (iota((256, 256), 1) // NB) % 8
    right = []
    for k in range(2):
        tall = exact(down, unpack_bands(bz[re * 2 + k]), NT)
        a = exact(tall, across.astype(f32))
        b = exact(tall, jnp.where(flip, minus, 0.0))
        right.append([split(jnp.where(same_mode, w, 0.0)) for w in (a, b)])

    def got2(off, carry):
        second(me, lax.rem(me + off, n_all)).wait_recv()
        return carry

    lax.fori_loop(1, n_all, got2, 0)
    data = D[...].astype(f32).reshape(n_all * 8, LANES).astype(bf16)
    both = dot16(left_both, data)
    summed = both[:128] + both[128:]
    groups = [
        summed[:, 0:256],
        summed[:, 256:512],
        jnp.concatenate([summed[:, 512:640], jnp.zeros((128, 128), f32)], axis=1),
    ]
    values = [[None, None], [None, None]]
    for k in range(2):
        total = None
        for c in range(2):
            x = jnp.concatenate(
                [g[((k * 2 + q) * 2 + c) * NB : ((k * 2 + q) * 2 + c + 1) * NB] for g in groups for q in range(2)],
                axis=0,
            )
            high, low = split(x)
            w_high, w_low = right[k][c]
            term = dot16(high, w_high) + dot16(low, w_high) + dot16(high, w_low)
            total = term if total is None else total + term
        for c in range(2):
            turned = group_swap(total[:, c * 128 : c * 128 + 128])
            for q in range(2):
                values[q][c] = (values[q][c] or []) + [
                    jnp.concatenate(
                        [
                            jnp.concatenate(
                                [turned[(g * 2 + q) * NB + h * 8 : (g * 2 + q) * NB + h * 8 + 8] for g in range(3)],
                                axis=0,
                            )
                            for h in range(2)
                        ],
                        axis=1,
                    )
                ]
    for q in range(2):
        xr = jnp.concatenate(values[q][0], axis=1)[:M]
        xi = jnp.concatenate(values[q][1], axis=1)[:M]
        er, ei = mode[q, :, 0, :], mode[q, :, 1, :]
        yr = exact(er, xr, TN) - exact(ei, xi, TN)
        yi = exact(er, xi, TN) + exact(ei, xr, TN)
        for k in range(2):
            at = (k * 2 + q) * M
            out[0, 0, at : at + M, 0:256] = yr[:, k * 256 : k * 256 + 256]
            out[0, 0, at : at + M, 256:512] = yi[:, k * 256 : k * 256 + 256]

    for off in range(1, n_kq):
        swap(kp, KP, 0, off).wait_send()
        swap(bz, BZ, 1, off).wait_send()

    def sent1(off, carry):
        first(lax.rem(re + off, n_re), re).wait_send()
        return carry

    lax.fori_loop(1, n_re, sent1, 0)

    def sent2(off, carry):
        second(lax.rem(me + off, n_all), me).wait_send()
        return carry

    lax.fori_loop(1, n_all, sent2, 0)


def fused(n_re, n_kq, couplings, re_vectors, degeneracy, kpoints, plus_index, mode_vectors, band_vectors):
    n_all = n_re * n_kq
    k_dev = kpoints.shape[0]
    vmem = pl.BlockSpec(memory_space=pltpu.VMEM)
    return pl.pallas_call(
        functools.partial(kernel, n_re, n_kq),
        out_shape=jax.ShapeDtypeStruct((1, 1, k_dev * Q * M // n_re, 2 * NB * NB), f32),
        in_specs=[pl.BlockSpec(memory_space=pltpu.HBM)] * 7,
        out_specs=vmem,
        scratch_shapes=[
            pltpu.VMEM((2, 4, M, Q, n_re * W), bf16),
            pltpu.SMEM((4, 3), jnp.int32),
            pltpu.SMEM((4,), jnp.int32),
            pltpu.VMEM((3, k_dev), jnp.int32),
            pltpu.SMEM((Q, k_dev), jnp.int32),
            pltpu.VMEM((Q, M, 2, M), f32),
            pltpu.VMEM((k_dev, 2, NB, W), f32),
            pltpu.VMEM((n_re * W // 128, M, 16, 128), f32),
            pltpu.VMEM((n_re, 16, LANES), bf16),
            pltpu.VMEM((n_re, 16, LANES), bf16),
            pltpu.VMEM((n_all, 8, LANES), bf16),
            pltpu.VMEM((n_all, 8, LANES), bf16),
            pltpu.VMEM((n_kq, k_dev, 8, 128), f32),
            pltpu.VMEM((n_kq, 8, 128), f32),
            pltpu.VMEM((k_dev, 8, 128), f32),
            pltpu.VMEM((8, 128), f32),
            pltpu.SemaphoreType.DMA((7,)),
            pltpu.SemaphoreType.DMA((n_re,)),
            pltpu.SemaphoreType.DMA((n_re,)),
            pltpu.SemaphoreType.DMA((n_all,)),
            pltpu.SemaphoreType.DMA((n_all,)),
            pltpu.SemaphoreType.DMA((2, n_kq)),
            pltpu.SemaphoreType.DMA((2, n_kq)),
        ],
        compiler_params=pltpu.CompilerParams(
            collective_id=0, has_side_effects=True, vmem_limit_bytes=60 * 1024 * 1024
        ),
    )(
        couplings.transpose(0, 1, 3, 2, 4),
        re_vectors,
        degeneracy,
        kpoints.T,
        plus_index.T,
        mode_vectors.transpose(0, 2, 1, 3),
        band_vectors.transpose(0, 1, 3, 2),
    )


def solution(mesh):
    n_re, n_kq = mesh.shape["re"], mesh.shape["kq"]
    body = functools.partial(fused, n_re, n_kq) if (n_re, n_kq) == (NB, W // NB) else shards
    return jax.shard_map(
        body,
        mesh=mesh,
        in_specs=(
            P(None, "re", None, None, None),
            P("re", None),
            P("re"),
            P("kq", None),
            P("kq", None),
            P(),
            P("kq", None, None, None),
        ),
        out_specs=P("kq", "re", None, None),
        check_vma=False,
    )
```

```python
import functools
import math

import jax
import jax.numpy as jnp
from jax import lax
from jax.experimental import pallas as pl
from jax.experimental.pallas import tpu as pltpu
from jax.sharding import PartitionSpec as P

W = 32
NB = 16
M = 18
Q = 2
NG = 16


precise = lax.Precision.HIGHEST


def phase_matrix(kint, rint, degen):
    product = jnp.sum(kint[:, None, :] * rint[None, :, :], axis=-1)
    angle = jnp.mod(product, NG).astype(jnp.float32) * (2.0 * math.pi / NG)
    weight = 1.0 / degen.astype(jnp.float32)
    cosine = jnp.cos(angle) * weight[None, :]
    sine = jnp.sin(angle) * weight[None, :]
    upper = jnp.concatenate([cosine, -sine], axis=1)
    lower = jnp.concatenate([sine, cosine], axis=1)
    return jnp.concatenate([upper, lower], axis=0).astype(jnp.bfloat16)


def phase_sum(kint, rint, degen, values):
    phases = phase_matrix(kint, rint, degen)
    lattice_count = values.shape[1]
    stacked = values.reshape(2 * lattice_count, -1)
    bloch = jnp.dot(phases, stacked, preferred_element_type=jnp.float32)
    return bloch.reshape(2, kint.shape[0], Q, M, -1)


def rotate_modes(real_part, imag_part, vectors):
    er = vectors[:, 0]
    ei = vectors[:, 1]
    out_real = jnp.einsum("qvu,kqvx->kqux", er, real_part, precision=precise) - jnp.einsum(
        "qvu,kqvx->kqux", ei, imag_part, precision=precise
    )
    out_imag = jnp.einsum("qvu,kqvx->kqux", er, imag_part, precision=precise) + jnp.einsum(
        "qvu,kqvx->kqux", ei, real_part, precision=precise
    )
    return (out_real, out_imag)


def project_right(real_part, imag_part, factor):
    fr = factor[:, 0]
    fi = factor[:, 1]
    out_real = jnp.einsum("rmn,rnj->rmj", real_part, fr, precision=precise) - jnp.einsum(
        "rmn,rnj->rmj", imag_part, fi, precision=precise
    )
    out_imag = jnp.einsum("rmn,rnj->rmj", real_part, fi, precision=precise) + jnp.einsum(
        "rmn,rnj->rmj", imag_part, fr, precision=precise
    )
    return jnp.stack([out_real, out_imag], axis=1)


def project_left(values, factor):
    fr = factor[:, 0]
    fi = factor[:, 1]
    xr = values[:, 0]
    xi = values[:, 1]
    out_real = jnp.einsum("rmi,rmj->rij", fr, xr, precision=precise) + jnp.einsum(
        "rmi,rmj->rij", fi, xi, precision=precise
    )
    out_imag = jnp.einsum("rmi,rmj->rij", fr, xi, precision=precise) - jnp.einsum(
        "rmi,rmj->rij", fi, xr, precision=precise
    )
    return jnp.stack([out_real, out_imag], axis=1)


def plus_bands(plus_index, band_vectors, pair_ids):
    targets = plus_index[pair_ids // Q, pair_ids % Q]
    every_band = lax.all_gather(band_vectors, "kq", axis=0, tiled=True)
    return every_band[targets]


def shards(couplings, re_vectors, degeneracy, kpoints, plus_index, mode_vectors, band_vectors):
    local_count = kpoints.shape[0]
    local_rows = local_count * Q * M
    share_rows = local_rows // lax.axis_size("re")
    share_pairs = share_rows // M
    share_ids = lax.axis_index("re") * share_rows + jnp.arange(share_rows, dtype=jnp.int32)
    pair_share = lax.axis_index("re") * share_pairs + jnp.arange(share_pairs, dtype=jnp.int32)
    local_share = jnp.arange(share_rows, dtype=jnp.int32) // M
    moved = lax.all_to_all(couplings, "re", split_axis=4, concat_axis=1, tiled=True)
    lattice_all, degen_all = (
        lax.all_gather(re_vectors, "re", axis=0, tiled=True),
        lax.all_gather(degeneracy, "re", axis=0, tiled=True),
    )
    columns = moved.shape[4]
    bloch = phase_sum(kpoints, lattice_all, degen_all, moved)
    moded_real, moded_imag = rotate_modes(bloch[0], bloch[1], mode_vectors)
    paired = jnp.stack([moded_real, moded_imag]).reshape(2, local_rows, columns)
    returned = lax.all_to_all(paired, "re", split_axis=1, concat_axis=2, tiled=True)
    right = project_right(
        returned[0].reshape(share_rows, W, W),
        returned[1].reshape(share_rows, W, W),
        band_vectors[share_ids // (Q * M)],
    )
    fetched = plus_bands(plus_index, band_vectors, pair_share)
    result = project_left(right, fetched[local_share])
    return result.reshape(1, 1, share_rows, 2 * NB * NB)


MESH = pl.DeviceIdType.MESH
LANES = 640
QUADS = ((4, 0, 1), (2, 3))
CHUNKS = ((0, 384), (384, 256))
f32 = jnp.float32
bf16 = jnp.bfloat16
NT = (((1,), (1,)), ((), ()))
TN = (((0,), (0,)), ((), ()))


def iota(shape, axis):
    return lax.broadcasted_iota(jnp.int32, shape, axis)


def exact(a, b, dims=(((1,), (0,)), ((), ()))):
    return lax.dot_general(a, b, dims, precision=precise, preferred_element_type=f32)


def split(a):
    high = a.astype(bf16)
    return high, (a - high.astype(f32)).astype(bf16)


def dot16(a, b):
    return jnp.dot(a, b, preferred_element_type=f32)


def unit_cosine(step):
    step = step - NG * jnp.floor(step * (1.0 / NG))
    fold = jnp.minimum(step, NG - step)
    near = jnp.minimum(fold, 8.0 - fold)
    size = jnp.where(near < 0.5, 1.0, jnp.where(near < 1.5, math.cos(math.pi / 8), math.cos(math.pi / 4)))
    size = jnp.where(near > 2.5, math.cos(3 * math.pi / 8), size)
    size = jnp.where(near > 3.5, 0.0, size)
    return jnp.where(fold > 4.5, -size, size)


def quarter_swap(parts):
    lane = iota(parts[0].shape, 1)
    upper = (lane & 64) != 0
    odd = (lane & 32) != 0
    stage = list(parts)
    for a, b in ((0, 2), (1, 3)):
        moved = pltpu.roll(jnp.where(upper, parts[a], parts[b]), 64, 1)
        stage[a] = jnp.where(upper, moved, parts[a])
        stage[b] = jnp.where(upper, parts[b], moved)
    out = list(stage)
    for a, b in ((0, 1), (2, 3)):
        out[a] = jnp.where(odd, pltpu.roll(stage[b], 32, 1), stage[a])
        out[b] = jnp.where(odd, stage[b], pltpu.roll(stage[a], 96, 1))
    return out


def group_swap(x):
    sub = iota(x.shape, 0)
    group = iota(x.shape, 1) // 16
    rows = x.shape[0]
    for s in (4, 2, 1):
        low_a = (sub & s) == 0
        low_b = (group & s) == 0
        down = pltpu.roll(pltpu.roll(x, rows - s, 0), 16 * s, 1)
        up = pltpu.roll(pltpu.roll(x, s, 0), 128 - 16 * s, 1)
        x = jnp.where(low_a == low_b, x, jnp.where(low_a, down, up))
    return x


def unpack_bands(tile):
    return jnp.concatenate([tile] + [pltpu.roll(tile, 128 - 32 * g, 1) for g in (1, 2, 3)], axis=0)


def kernel(
    n_re, n_kq, coup_any, rvec_any, degen_any, kp_any, plus_any, mode_any, bands_any, out,
    coup, rvec, degen_own, kp_own, plus, mode, bands,
    F, Y, X, S, D, BZ, KP, bz, kp, fetch, send1, recv1, send2, recv2, sendb, recvb,
):
    re = lax.axis_index("re")
    kq = lax.axis_index("kq")
    n_all = n_re * n_kq
    me = kq * n_re + re
    width = n_re * W
    tiles = width // 128
    mine = pl.ds(pl.multiple_of(kq * width, width), width)
    pairs = [
        (coup_any.at[:, :, :, :, mine], coup),
        (rvec_any, rvec),
        (degen_any, degen_own),
        (kp_any, kp_own),
        (bands_any, bands),
        (plus_any, plus),
        (mode_any, mode),
    ]
    loads = [pltpu.make_async_copy(a, b, fetch.at[n]) for n, (a, b) in enumerate(pairs)]
    for load in loads:
        load.start()
    barrier = pltpu.get_barrier_semaphore()

    def hello(off, carry):
        to = lax.rem(me + off, n_all)
        pl.semaphore_signal(
            barrier, inc=1, device_id=(lax.rem(to, n_re), to // n_re), device_id_type=MESH
        )
        return carry

    lax.fori_loop(1, n_all, hello, 0)

    for n in range(4):
        loads[n].wait()
    kp[...] = jnp.zeros_like(kp)
    kp[0:3, 0 : kp_own.shape[1]] = kp_own[...].astype(f32)
    row = iota((16, 128), 0) // 2 % 4
    lane = iota((16, 128), 1)
    spare = jnp.zeros((16, 128), f32)
    for r in range(4):
        for d in range(4):
            value = (rvec[r, d] if d < 3 else degen_own[r]).astype(f32)
            spare = jnp.where((row == r) & (lane == 64 + d), value, spare)
    def first(to, frm, part):
        lanes = pl.ds(*CHUNKS[part])
        return pltpu.make_async_remote_copy(
            src_ref=Y.at[to, :, lanes], dst_ref=X.at[frm, :, lanes],
            send_sem=send1.at[part, to], recv_sem=recv1.at[part, frm],
            device_id=(to, kq), device_id_type=MESH,
        )

    def swap(ref, full, s, off):
        other = lax.rem(kq + off, n_kq)
        return pltpu.make_async_remote_copy(
            src_ref=ref, dst_ref=full.at[kq],
            send_sem=sendb.at[s, other], recv_sem=recvb.at[s, kq],
            device_id=(re, other), device_id_type=MESH,
        )

    def swapped(ref, full, s, off):
        other = lax.rem(kq + off, n_kq)
        return pltpu.make_async_remote_copy(
            src_ref=ref, dst_ref=full.at[other],
            send_sem=sendb.at[s, other], recv_sem=recvb.at[s, other],
            device_id=(re, other), device_id_type=MESH,
        )

    for part, quads in enumerate(QUADS):
        for t in range(tiles):
            for v4 in quads:
                count = min(4, M - 4 * v4)
                for a in range(8):
                    F[t, 4 * v4 : 4 * v4 + count, 2 * a : 2 * a + 2, :] = coup[
                        a // 4, a % 4, 4 * v4 : 4 * v4 + count, :, t * 128 : t * 128 + 128
                    ].astype(f32)
                parts = [F[t, 4 * v4 + v] if v < count else jnp.zeros((16, 128), f32) for v in range(4)]
                moved = quarter_swap(parts)
                at = (v4 + 1) % 5 * 128
                for m in range(4):
                    piece = moved[m] + spare if v4 == 4 else moved[m]
                    Y[t * 4 + m, :, at : at + 128] = piece.astype(bf16)
        if part == 0:
            pl.semaphore_wait(barrier, n_all - 1)
            for off in range(1, n_kq):
                swap(kp, KP, 0, off).start()

        def go1(off, carry, part=part):
            first(lax.rem(re + off, n_re), re, part).start()
            return carry

        lax.fori_loop(1, n_re, go1, 0)
    loads[4].wait()
    for g in range(4):
        bz[:, :, g * 32 : g * 32 + 32] = bands[:, g // 2, g % 2 * 8 : g % 2 * 8 + 8, :]
    for off in range(1, n_kq):
        swap(bz, BZ, 1, off).start()
    loads[5].wait()
    loads[6].wait()
    X[re] = Y[re]
    KP[kq] = kp[...]
    BZ[kq] = bz[...]
    for off in range(1, n_kq):
        swapped(kp, KP, 0, off).wait_recv()
    n_dev = bz.shape[0]
    rows = n_kq * n_dev * 4
    points = KP[0]
    for other in range(1, n_kq):
        points = points + pltpu.roll(KP[other], other * n_dev, 1)
    points = jnp.concatenate([jnp.zeros((64, 128), f32), points, jnp.zeros((56, 128), f32)], axis=0)
    pick = ((iota((rows, 128), 0) // 4) == iota((rows, 128), 1)).astype(bf16)
    grid = lax.dot_general(pick, points.astype(bf16), NT, preferred_element_type=f32).astype(bf16)

    def got1(off, carry, part=0):
        first(re, lax.rem(re + off, n_re), part).wait_recv()
        return carry

    lax.fori_loop(1, n_re, got1, 0)
    depth = n_re * 16
    lattice = X[:, :, 0:128].reshape(depth, 128)
    product = lax.dot_general(grid, lattice, NT, preferred_element_type=f32)
    ones = (iota((rows, 128), 1) == 67).astype(bf16)
    degen = lax.dot_general(ones, lattice, NT, preferred_element_type=f32)
    row = iota((rows, depth), 0)
    col = iota((rows, depth), 1)
    turn = (((col // 8) & 1) - (row & 1)).astype(f32) * 4.0
    same = ((row // 2) & 1) == (col & 1)
    phases = jnp.where(same, unit_cosine(product + turn) * (1.0 / degen), 0.0).astype(bf16)

    def second(to, frm, part):
        lanes = pl.ds(*CHUNKS[part])
        return pltpu.make_async_remote_copy(
            src_ref=S.at[to, :, lanes], dst_ref=D.at[frm, :, lanes],
            send_sem=send2.at[part, to], recv_sem=recv2.at[part, frm],
            device_id=(lax.rem(to, n_re), to // n_re), device_id_type=MESH,
        )

    def sum_and_send(part):
        start, count = CHUNKS[part]
        for at in range(start, start + count, 128):
            bloch = dot16(phases, X[:, :, at : at + 128].reshape(depth, 128))
            S[:, :, at : at + 128] = bloch.reshape(n_all, 8, 128).astype(bf16)

        def go2(off, carry):
            second(lax.rem(me + off, n_all), me, part).start()
            return carry

        lax.fori_loop(1, n_all, go2, 0)

    sum_and_send(0)

    down = ((iota((256, 128), 0) & 31) == iota((256, 128), 1)).astype(f32)
    lane = iota((32, 256), 1)
    across = iota((32, 256), 0) == (lane // 128) * NB + (lane & 15)
    flip = iota((32, 256), 0) == (1 - lane // 128) * NB + (lane & 15)
    minus = jnp.where(lane < 128, -1.0, 1.0)
    same_mode = iota((256, 256), 0) // 32 == (iota((256, 256), 1) // NB) % 8
    right = []
    for k in range(2):
        tall = exact(down, unpack_bands(bz[re * 2 + k]), NT)
        a = exact(tall, across.astype(f32))
        b = exact(tall, jnp.where(flip, minus, 0.0))
        right.append([split(jnp.where(same_mode, w, 0.0)) for w in (a, b)])

    lax.fori_loop(1, n_re, functools.partial(got1, part=1), 0)
    sum_and_send(1)
    D[me] = S[me]

    for off in range(1, n_kq):
        swapped(bz, BZ, 1, off).wait_recv()
    spread = (iota((128, 256), 0) == iota((128, 256), 1) // 8).astype(f32)
    lane = iota((NB, 256), 1)
    imag_in = (lane & 1) == 1
    left = []
    for p in range(4):
        target = plus[p % 2, re * 2 + p // 2]
        tile = BZ[target // n_dev, lax.rem(target, n_dev)]
        wide = exact(unpack_bands(tile), spread)
        real, imag = wide[:NB], wide[NB:]
        own = ((lane // 2) & 3) == p
        left.append(jnp.where(own, jnp.where(imag_in, imag, real), 0.0))
        left.append(jnp.where(own, jnp.where(imag_in, real, -imag), 0.0))
    left_high, left_low = split(jnp.concatenate(left, axis=0))
    left_both = jnp.concatenate([left_high, left_low], axis=0)
    pieces = [[{} for c in range(2)] for q in range(2)]
    for part, (start, count) in enumerate(CHUNKS):

        def got2(off, carry, part=part):
            second(me, lax.rem(me + off, n_all), part).wait_recv()
            return carry

        lax.fori_loop(1, n_all, got2, 0)
        data = D[:, :, start : start + count].astype(f32).reshape(n_all * 8, count).astype(bf16)
        both = dot16(left_both, data)
        summed = both[:128] + both[128:]
        if part == 0:
            groups = {
                0: summed[:, 128:384],
                2: jnp.concatenate([summed[:, 0:128], jnp.zeros((128, 128), f32)], axis=1),
            }
        else:
            groups = {1: summed}
        for k in range(2):
            total = None
            for c in range(2):
                x = jnp.concatenate(
                    [
                        g[((k * 2 + q) * 2 + c) * NB : ((k * 2 + q) * 2 + c + 1) * NB]
                        for g in groups.values()
                        for q in range(2)
                    ],
                    axis=0,
                )
                high, low = split(x)
                w_high, w_low = right[k][c]
                term = dot16(high, w_high) + dot16(low, w_high) + dot16(high, w_low)
                total = term if total is None else total + term
            for c in range(2):
                turned = group_swap(total[:, c * 128 : c * 128 + 128])
                for n, g in enumerate(groups):
                    for q in range(2):
                        for h in range(2):
                            at = (n * 2 + q) * NB + h * 8
                            pieces[q][c][g, k, h] = turned[at : at + 8]
    values = [
        [
            jnp.concatenate(
                [
                    jnp.concatenate([pieces[q][c][g, k, h] for g in range(3)], axis=0)
                    for k in range(2)
                    for h in range(2)
                ],
                axis=1,
            )
            for c in range(2)
        ]
        for q in range(2)
    ]
    for q in range(2):
        xr = values[q][0][:M]
        xi = values[q][1][:M]
        er, ei = mode[q, :, 0, :], mode[q, :, 1, :]
        yr = exact(er, xr, TN) - exact(ei, xi, TN)
        yi = exact(er, xi, TN) + exact(ei, xr, TN)
        for k in range(2):
            at = (k * 2 + q) * M
            out[0, 0, at : at + M, 0:256] = yr[:, k * 256 : k * 256 + 256]
            out[0, 0, at : at + M, 256:512] = yi[:, k * 256 : k * 256 + 256]

    for off in range(1, n_kq):
        swap(kp, KP, 0, off).wait_send()
        swap(bz, BZ, 1, off).wait_send()

    for part in range(2):

        def sent1(off, carry, part=part):
            first(lax.rem(re + off, n_re), re, part).wait_send()
            return carry

        def sent2(off, carry, part=part):
            second(lax.rem(me + off, n_all), me, part).wait_send()
            return carry

        lax.fori_loop(1, n_re, sent1, 0)
        lax.fori_loop(1, n_all, sent2, 0)


def fused(n_re, n_kq, couplings, re_vectors, degeneracy, kpoints, plus_index, mode_vectors, band_vectors):
    n_all = n_re * n_kq
    k_dev = kpoints.shape[0]
    vmem = pl.BlockSpec(memory_space=pltpu.VMEM)
    return pl.pallas_call(
        functools.partial(kernel, n_re, n_kq),
        out_shape=jax.ShapeDtypeStruct((1, 1, k_dev * Q * M // n_re, 2 * NB * NB), f32),
        in_specs=[pl.BlockSpec(memory_space=pltpu.HBM)] * 7,
        out_specs=vmem,
        scratch_shapes=[
            pltpu.VMEM((2, 4, M, Q, n_re * W), bf16),
            pltpu.SMEM((4, 3), jnp.int32),
            pltpu.SMEM((4,), jnp.int32),
            pltpu.VMEM((3, k_dev), jnp.int32),
            pltpu.SMEM((Q, k_dev), jnp.int32),
            pltpu.VMEM((Q, M, 2, M), f32),
            pltpu.VMEM((k_dev, 2, NB, W), f32),
            pltpu.VMEM((n_re * W // 128, M, 16, 128), f32),
            pltpu.VMEM((n_re, 16, LANES), bf16),
            pltpu.VMEM((n_re, 16, LANES), bf16),
            pltpu.VMEM((n_all, 8, LANES), bf16),
            pltpu.VMEM((n_all, 8, LANES), bf16),
            pltpu.VMEM((n_kq, k_dev, 8, 128), f32),
            pltpu.VMEM((n_kq, 8, 128), f32),
            pltpu.VMEM((k_dev, 8, 128), f32),
            pltpu.VMEM((8, 128), f32),
            pltpu.SemaphoreType.DMA((7,)),
            pltpu.SemaphoreType.DMA((2, n_re)),
            pltpu.SemaphoreType.DMA((2, n_re)),
            pltpu.SemaphoreType.DMA((2, n_all)),
            pltpu.SemaphoreType.DMA((2, n_all)),
            pltpu.SemaphoreType.DMA((2, n_kq)),
            pltpu.SemaphoreType.DMA((2, n_kq)),
        ],
        compiler_params=pltpu.CompilerParams(
            collective_id=0, has_side_effects=True, vmem_limit_bytes=60 * 1024 * 1024
        ),
    )(
        couplings.transpose(0, 1, 3, 2, 4),
        re_vectors,
        degeneracy,
        kpoints.T,
        plus_index.T,
        mode_vectors.transpose(0, 2, 1, 3),
        band_vectors.transpose(0, 1, 3, 2),
    )


def solution(mesh):
    n_re, n_kq = mesh.shape["re"], mesh.shape["kq"]
    body = functools.partial(fused, n_re, n_kq) if (n_re, n_kq) == (NB, W // NB) else shards
    return jax.shard_map(
        body,
        mesh=mesh,
        in_specs=(
            P(None, "re", None, None, None),
            P("re", None),
            P("re"),
            P("kq", None),
            P("kq", None),
            P(),
            P("kq", None, None, None),
        ),
        out_specs=P("kq", "re", None, None),
        check_vma=False,
    )
```

```python
import functools
import math

import jax
import jax.numpy as jnp
from jax import lax
from jax.experimental import pallas as pl
from jax.experimental.pallas import tpu as pltpu
from jax.sharding import PartitionSpec as P

W = 32
NB = 16
M = 18
Q = 2
NG = 16


precise = lax.Precision.HIGHEST


def phase_matrix(kint, rint, degen):
    product = jnp.sum(kint[:, None, :] * rint[None, :, :], axis=-1)
    angle = jnp.mod(product, NG).astype(jnp.float32) * (2.0 * math.pi / NG)
    weight = 1.0 / degen.astype(jnp.float32)
    cosine = jnp.cos(angle) * weight[None, :]
    sine = jnp.sin(angle) * weight[None, :]
    upper = jnp.concatenate([cosine, -sine], axis=1)
    lower = jnp.concatenate([sine, cosine], axis=1)
    return jnp.concatenate([upper, lower], axis=0).astype(jnp.bfloat16)


def phase_sum(kint, rint, degen, values):
    phases = phase_matrix(kint, rint, degen)
    lattice_count = values.shape[1]
    stacked = values.reshape(2 * lattice_count, -1)
    bloch = jnp.dot(phases, stacked, preferred_element_type=jnp.float32)
    return bloch.reshape(2, kint.shape[0], Q, M, -1)


def rotate_modes(real_part, imag_part, vectors):
    er = vectors[:, 0]
    ei = vectors[:, 1]
    out_real = jnp.einsum("qvu,kqvx->kqux", er, real_part, precision=precise) - jnp.einsum(
        "qvu,kqvx->kqux", ei, imag_part, precision=precise
    )
    out_imag = jnp.einsum("qvu,kqvx->kqux", er, imag_part, precision=precise) + jnp.einsum(
        "qvu,kqvx->kqux", ei, real_part, precision=precise
    )
    return (out_real, out_imag)


def project_right(real_part, imag_part, factor):
    fr = factor[:, 0]
    fi = factor[:, 1]
    out_real = jnp.einsum("rmn,rnj->rmj", real_part, fr, precision=precise) - jnp.einsum(
        "rmn,rnj->rmj", imag_part, fi, precision=precise
    )
    out_imag = jnp.einsum("rmn,rnj->rmj", real_part, fi, precision=precise) + jnp.einsum(
        "rmn,rnj->rmj", imag_part, fr, precision=precise
    )
    return jnp.stack([out_real, out_imag], axis=1)


def project_left(values, factor):
    fr = factor[:, 0]
    fi = factor[:, 1]
    xr = values[:, 0]
    xi = values[:, 1]
    out_real = jnp.einsum("rmi,rmj->rij", fr, xr, precision=precise) + jnp.einsum(
        "rmi,rmj->rij", fi, xi, precision=precise
    )
    out_imag = jnp.einsum("rmi,rmj->rij", fr, xi, precision=precise) - jnp.einsum(
        "rmi,rmj->rij", fi, xr, precision=precise
    )
    return jnp.stack([out_real, out_imag], axis=1)


def plus_bands(plus_index, band_vectors, pair_ids):
    targets = plus_index[pair_ids // Q, pair_ids % Q]
    every_band = lax.all_gather(band_vectors, "kq", axis=0, tiled=True)
    return every_band[targets]


def shards(couplings, re_vectors, degeneracy, kpoints, plus_index, mode_vectors, band_vectors):
    local_count = kpoints.shape[0]
    local_rows = local_count * Q * M
    share_rows = local_rows // lax.axis_size("re")
    share_pairs = share_rows // M
    share_ids = lax.axis_index("re") * share_rows + jnp.arange(share_rows, dtype=jnp.int32)
    pair_share = lax.axis_index("re") * share_pairs + jnp.arange(share_pairs, dtype=jnp.int32)
    local_share = jnp.arange(share_rows, dtype=jnp.int32) // M
    moved = lax.all_to_all(couplings, "re", split_axis=4, concat_axis=1, tiled=True)
    lattice_all, degen_all = (
        lax.all_gather(re_vectors, "re", axis=0, tiled=True),
        lax.all_gather(degeneracy, "re", axis=0, tiled=True),
    )
    columns = moved.shape[4]
    bloch = phase_sum(kpoints, lattice_all, degen_all, moved)
    moded_real, moded_imag = rotate_modes(bloch[0], bloch[1], mode_vectors)
    paired = jnp.stack([moded_real, moded_imag]).reshape(2, local_rows, columns)
    returned = lax.all_to_all(paired, "re", split_axis=1, concat_axis=2, tiled=True)
    right = project_right(
        returned[0].reshape(share_rows, W, W),
        returned[1].reshape(share_rows, W, W),
        band_vectors[share_ids // (Q * M)],
    )
    fetched = plus_bands(plus_index, band_vectors, pair_share)
    result = project_left(right, fetched[local_share])
    return result.reshape(1, 1, share_rows, 2 * NB * NB)


MESH = pl.DeviceIdType.MESH
LANES = 640
GEO = 576
f32 = jnp.float32
bf16 = jnp.bfloat16
NT = (((1,), (1,)), ((), ()))
TN = (((0,), (0,)), ((), ()))


def iota(shape, axis):
    return lax.broadcasted_iota(jnp.int32, shape, axis)


def exact(a, b, dims=(((1,), (0,)), ((), ()))):
    return lax.dot_general(a, b, dims, precision=precise, preferred_element_type=f32)


def split(a):
    high = a.astype(bf16)
    return high, (a - high.astype(f32)).astype(bf16)


def dot16(a, b):
    return jnp.dot(a, b, preferred_element_type=f32)


def unit_cosine(step):
    step = step - NG * jnp.floor(step * (1.0 / NG))
    fold = jnp.minimum(step, NG - step)
    near = jnp.minimum(fold, 8.0 - fold)
    size = jnp.where(near < 0.5, 1.0, jnp.where(near < 1.5, math.cos(math.pi / 8), math.cos(math.pi / 4)))
    size = jnp.where(near > 2.5, math.cos(3 * math.pi / 8), size)
    size = jnp.where(near > 3.5, 0.0, size)
    return jnp.where(fold > 4.5, -size, size)


def quarter_swap(parts):
    lane = iota(parts[0].shape, 1)
    upper = (lane & 64) != 0
    odd = (lane & 32) != 0
    stage = list(parts)
    for a, b in ((0, 2), (1, 3)):
        moved = pltpu.roll(jnp.where(upper, parts[a], parts[b]), 64, 1)
        stage[a] = jnp.where(upper, moved, parts[a])
        stage[b] = jnp.where(upper, parts[b], moved)
    out = list(stage)
    for a, b in ((0, 1), (2, 3)):
        out[a] = jnp.where(odd, pltpu.roll(stage[b], 32, 1), stage[a])
        out[b] = jnp.where(odd, stage[b], pltpu.roll(stage[a], 96, 1))
    return out


def group_swap(x):
    sub = iota(x.shape, 0)
    group = iota(x.shape, 1) // 16
    rows = x.shape[0]
    for s in (4, 2, 1):
        low_a = (sub & s) == 0
        low_b = (group & s) == 0
        down = pltpu.roll(pltpu.roll(x, rows - s, 0), 16 * s, 1)
        up = pltpu.roll(pltpu.roll(x, s, 0), 128 - 16 * s, 1)
        x = jnp.where(low_a == low_b, x, jnp.where(low_a, down, up))
    return x


def unpack_bands(tile):
    return jnp.concatenate([tile] + [pltpu.roll(tile, 128 - 32 * g, 1) for g in (1, 2, 3)], axis=0)


def kernel(
    n_re, n_kq, coup_any, rvec_any, degen_any, kp_any, plus_any, mode_any, bands_any, out,
    coup, rvec, degen_own, kp_own, plus, mode, bands,
    F, Y, X, S, D, BZ, KP, bz, kp, fetch, send1, recv1, send2, recv2, sendb, recvb,
):
    re = lax.axis_index("re")
    kq = lax.axis_index("kq")
    n_all = n_re * n_kq
    me = kq * n_re + re
    width = n_re * W
    tiles = width // 128
    mine = pl.ds(pl.multiple_of(kq * width, width), width)
    pairs = [
        (coup_any.at[:, :, :, :, mine], coup),
        (rvec_any, rvec),
        (degen_any, degen_own),
        (kp_any, kp_own),
        (bands_any, bands),
        (plus_any, plus),
        (mode_any, mode),
    ]
    loads = [pltpu.make_async_copy(a, b, fetch.at[n]) for n, (a, b) in enumerate(pairs)]
    for load in loads:
        load.start()
    barrier = pltpu.get_barrier_semaphore()

    for off in range(1, n_all):
        to = lax.rem(me + off, n_all)
        pl.semaphore_signal(
            barrier, inc=1, device_id=(lax.rem(to, n_re), to // n_re), device_id_type=MESH
        )

    for n in range(4):
        loads[n].wait()
    kp[...] = jnp.zeros_like(kp)
    kp[0:3, 0 : kp_own.shape[1]] = kp_own[...].astype(f32)
    row = iota((16, 128), 0) // 2 % 4
    lane = iota((16, 128), 1)
    spare = jnp.zeros((16, 128), f32)
    for r in range(4):
        for d in range(4):
            value = (rvec[r, d] if d < 3 else degen_own[r]).astype(f32)
            spare = jnp.where((row == r) & (lane == 64 + d), value, spare)
    for t in range(tiles):
        for a in range(8):
            F[t, :, 2 * a : 2 * a + 2, :] = coup[a // 4, a % 4, :, :, t * 128 : t * 128 + 128].astype(f32)
        for v4 in range(5):
            parts = []
            for v in range(4 * v4, 4 * v4 + 4):
                parts.append(F[t, v] if v < M else jnp.zeros((16, 128), f32))
            moved = quarter_swap(parts)
            for m in range(4):
                piece = moved[m] + spare if v4 == 4 else moved[m]
                Y[t * 4 + m, :, v4 * 128 : v4 * 128 + 128] = piece.astype(bf16)

    pl.semaphore_wait(barrier, n_all - 1)

    def first(to, frm):
        return pltpu.make_async_remote_copy(
            src_ref=Y.at[to], dst_ref=X.at[frm],
            send_sem=send1, recv_sem=recv1,
            device_id=(to, kq), device_id_type=MESH,
        )

    def swap(ref, full, s, off):
        other = lax.rem(kq + off, n_kq)
        return pltpu.make_async_remote_copy(
            src_ref=ref, dst_ref=full.at[kq],
            send_sem=sendb.at[s, other], recv_sem=recvb.at[s, kq],
            device_id=(re, other), device_id_type=MESH,
        )

    def swapped(ref, full, s, off):
        other = lax.rem(kq + off, n_kq)
        return pltpu.make_async_remote_copy(
            src_ref=ref, dst_ref=full.at[other],
            send_sem=sendb.at[s, other], recv_sem=recvb.at[s, other],
            device_id=(re, other), device_id_type=MESH,
        )

    for off in range(1, n_kq):
        swap(kp, KP, 0, off).start()

    for off in range(1, n_re):
        first(lax.rem(re + off, n_re), re).start()
    loads[4].wait()
    for g in range(4):
        bz[:, :, g * 32 : g * 32 + 32] = bands[:, g // 2, g % 2 * 8 : g % 2 * 8 + 8, :]
    for off in range(1, n_kq):
        swap(bz, BZ, 1, off).start()
    loads[5].wait()
    loads[6].wait()
    X[re] = Y[re]
    KP[kq] = kp[...]
    BZ[kq] = bz[...]
    for off in range(1, n_kq):
        swapped(kp, KP, 0, off).wait_recv()
    n_dev = bz.shape[0]
    rows = n_kq * n_dev * 4
    points = KP[0]
    for other in range(1, n_kq):
        points = points + pltpu.roll(KP[other], other * n_dev, 1)
    points = jnp.concatenate([jnp.zeros((64, 128), f32), points, jnp.zeros((56, 128), f32)], axis=0)
    pick = ((iota((rows, 128), 0) // 4) == iota((rows, 128), 1)).astype(bf16)
    grid = lax.dot_general(pick, points.astype(bf16), NT, preferred_element_type=f32).astype(bf16)

    every1 = pltpu.make_async_remote_copy(
        src_ref=Y.at[0 : n_re - 1], dst_ref=X.at[0 : n_re - 1], send_sem=send1, recv_sem=recv1,
        device_id=(lax.rem(re + 1, n_re), kq), device_id_type=MESH,
    )
    every1.wait_recv()
    depth = n_re * 16
    lattice = X[:, :, 512:640].reshape(depth, 128)
    product = lax.dot_general(grid, lattice, NT, preferred_element_type=f32)
    ones = (iota((rows, 128), 1) == 67).astype(bf16)
    degen = lax.dot_general(ones, lattice, NT, preferred_element_type=f32)
    row = iota((rows, depth), 0)
    col = iota((rows, depth), 1)
    turn = (((col // 8) & 1) - (row & 1)).astype(f32) * 4.0
    same = ((row // 2) & 1) == (col & 1)
    phases = jnp.where(same, unit_cosine(product + turn) * (1.0 / degen), 0.0).astype(bf16)
    for t in range(5):
        lanes = slice(t * 128, t * 128 + 128)
        bloch = dot16(phases, X[:, :, lanes].reshape(depth, 128))
        S[:, :, lanes] = bloch.reshape(n_all, 8, 128).astype(bf16)

    def second(to, frm):
        return pltpu.make_async_remote_copy(
            src_ref=S.at[to], dst_ref=D.at[frm],
            send_sem=send2, recv_sem=recv2,
            device_id=(lax.rem(to, n_re), to // n_re), device_id_type=MESH,
        )

    for off in range(1, n_all):
        second(lax.rem(me + off, n_all), me).start()
    D[me] = S[me]

    for off in range(1, n_kq):
        swapped(bz, BZ, 1, off).wait_recv()
    spread = (iota((128, 256), 0) == iota((128, 256), 1) // 8).astype(f32)
    lane = iota((NB, 256), 1)
    imag_in = (lane & 1) == 1
    left = []
    for p in range(4):
        target = plus[p % 2, re * 2 + p // 2]
        tile = BZ[target // n_dev, lax.rem(target, n_dev)]
        wide = exact(unpack_bands(tile), spread)
        real, imag = wide[:NB], wide[NB:]
        own = ((lane // 2) & 3) == p
        left.append(jnp.where(own, jnp.where(imag_in, imag, real), 0.0))
        left.append(jnp.where(own, jnp.where(imag_in, real, -imag), 0.0))
    left_high, left_low = split(jnp.concatenate(left, axis=0))
    left_both = jnp.concatenate([left_high, left_low], axis=0)
    down = ((iota((256, 128), 0) & 31) == iota((256, 128), 1)).astype(f32)
    lane = iota((32, 256), 1)
    across = iota((32, 256), 0) == (lane // 128) * NB + (lane & 15)
    flip = iota((32, 256), 0) == (1 - lane // 128) * NB + (lane & 15)
    minus = jnp.where(lane < 128, -1.0, 1.0)
    same_mode = iota((256, 256), 0) // 32 == (iota((256, 256), 1) // NB) % 8
    right = []
    for k in range(2):
        tall = exact(down, unpack_bands(bz[re * 2 + k]), NT)
        a = exact(tall, across.astype(f32))
        b = exact(tall, jnp.where(flip, minus, 0.0))
        right.append([split(jnp.where(same_mode, w, 0.0)) for w in (a, b)])

    every2 = pltpu.make_async_remote_copy(
        src_ref=S.at[0 : n_all - 1], dst_ref=D.at[0 : n_all - 1], send_sem=send2, recv_sem=recv2,
        device_id=(lax.rem(re + 1, n_re), kq), device_id_type=MESH,
    )
    every2.wait_recv()
    data = D[...].astype(f32).reshape(n_all * 8, LANES).astype(bf16)
    both = dot16(left_both, data)
    summed = both[:128] + both[128:]
    groups = [
        summed[:, 0:256],
        summed[:, 256:512],
        jnp.concatenate([summed[:, 512:640], jnp.zeros((128, 128), f32)], axis=1),
    ]
    values = [[None, None], [None, None]]
    for k in range(2):
        total = None
        for c in range(2):
            x = jnp.concatenate(
                [g[((k * 2 + q) * 2 + c) * NB : ((k * 2 + q) * 2 + c + 1) * NB] for g in groups for q in range(2)],
                axis=0,
            )
            high, low = split(x)
            w_high, w_low = right[k][c]
            term = dot16(high, w_high) + dot16(low, w_high) + dot16(high, w_low)
            total = term if total is None else total + term
        for c in range(2):
            turned = group_swap(total[:, c * 128 : c * 128 + 128])
            for q in range(2):
                values[q][c] = (values[q][c] or []) + [
                    jnp.concatenate(
                        [
                            jnp.concatenate(
                                [turned[(g * 2 + q) * NB + h * 8 : (g * 2 + q) * NB + h * 8 + 8] for g in range(3)],
                                axis=0,
                            )
                            for h in range(2)
                        ],
                        axis=1,
                    )
                ]
    for q in range(2):
        xr = jnp.concatenate(values[q][0], axis=1)[:M]
        xi = jnp.concatenate(values[q][1], axis=1)[:M]
        er, ei = mode[q, :, 0, :], mode[q, :, 1, :]
        yr = exact(er, xr, TN) - exact(ei, xi, TN)
        yi = exact(er, xi, TN) + exact(ei, xr, TN)
        for k in range(2):
            at = (k * 2 + q) * M
            out[0, 0, at : at + M, 0:256] = yr[:, k * 256 : k * 256 + 256]
            out[0, 0, at : at + M, 256:512] = yi[:, k * 256 : k * 256 + 256]

    for off in range(1, n_kq):
        swap(kp, KP, 0, off).wait_send()
        swap(bz, BZ, 1, off).wait_send()

    every1.wait_send()
    every2.wait_send()


def fused(n_re, n_kq, couplings, re_vectors, degeneracy, kpoints, plus_index, mode_vectors, band_vectors):
    n_all = n_re * n_kq
    k_dev = kpoints.shape[0]
    vmem = pl.BlockSpec(memory_space=pltpu.VMEM)
    return pl.pallas_call(
        functools.partial(kernel, n_re, n_kq),
        out_shape=jax.ShapeDtypeStruct((1, 1, k_dev * Q * M // n_re, 2 * NB * NB), f32),
        in_specs=[pl.BlockSpec(memory_space=pltpu.HBM)] * 7,
        out_specs=vmem,
        scratch_shapes=[
            pltpu.VMEM((2, 4, M, Q, n_re * W), bf16),
            pltpu.SMEM((4, 3), jnp.int32),
            pltpu.SMEM((4,), jnp.int32),
            pltpu.VMEM((3, k_dev), jnp.int32),
            pltpu.SMEM((Q, k_dev), jnp.int32),
            pltpu.VMEM((Q, M, 2, M), f32),
            pltpu.VMEM((k_dev, 2, NB, W), f32),
            pltpu.VMEM((n_re * W // 128, M, 16, 128), f32),
            pltpu.VMEM((n_re, 16, LANES), bf16),
            pltpu.VMEM((n_re, 16, LANES), bf16),
            pltpu.VMEM((n_all, 8, LANES), bf16),
            pltpu.VMEM((n_all, 8, LANES), bf16),
            pltpu.VMEM((n_kq, k_dev, 8, 128), f32),
            pltpu.VMEM((n_kq, 8, 128), f32),
            pltpu.VMEM((k_dev, 8, 128), f32),
            pltpu.VMEM((8, 128), f32),
            pltpu.SemaphoreType.DMA((7,)),
            pltpu.SemaphoreType.DMA,
            pltpu.SemaphoreType.DMA,
            pltpu.SemaphoreType.DMA,
            pltpu.SemaphoreType.DMA,
            pltpu.SemaphoreType.DMA((2, n_kq)),
            pltpu.SemaphoreType.DMA((2, n_kq)),
        ],
        compiler_params=pltpu.CompilerParams(
            collective_id=0, has_side_effects=True, vmem_limit_bytes=60 * 1024 * 1024
        ),
    )(
        couplings.transpose(0, 1, 3, 2, 4),
        re_vectors,
        degeneracy,
        kpoints.T,
        plus_index.T,
        mode_vectors.transpose(0, 2, 1, 3),
        band_vectors.transpose(0, 1, 3, 2),
    )


def solution(mesh):
    n_re, n_kq = mesh.shape["re"], mesh.shape["kq"]
    body = functools.partial(fused, n_re, n_kq) if (n_re, n_kq) == (NB, W // NB) else shards
    return jax.shard_map(
        body,
        mesh=mesh,
        in_specs=(
            P(None, "re", None, None, None),
            P("re", None),
            P("re"),
            P("kq", None),
            P("kq", None),
            P(),
            P("kq", None, None, None),
        ),
        out_specs=P("kq", "re", None, None),
        check_vma=False,
    )
```

```python
import functools
import math

import jax
import jax.numpy as jnp
from jax import lax
from jax.experimental import pallas as pl
from jax.experimental.pallas import tpu as pltpu
from jax.sharding import PartitionSpec as P

W = 32
NB = 16
M = 18
Q = 2
NG = 16


precise = lax.Precision.HIGHEST


def phase_matrix(kint, rint, degen):
    product = jnp.sum(kint[:, None, :] * rint[None, :, :], axis=-1)
    angle = jnp.mod(product, NG).astype(jnp.float32) * (2.0 * math.pi / NG)
    weight = 1.0 / degen.astype(jnp.float32)
    cosine = jnp.cos(angle) * weight[None, :]
    sine = jnp.sin(angle) * weight[None, :]
    upper = jnp.concatenate([cosine, -sine], axis=1)
    lower = jnp.concatenate([sine, cosine], axis=1)
    return jnp.concatenate([upper, lower], axis=0).astype(jnp.bfloat16)


def phase_sum(kint, rint, degen, values):
    phases = phase_matrix(kint, rint, degen)
    lattice_count = values.shape[1]
    stacked = values.reshape(2 * lattice_count, -1)
    bloch = jnp.dot(phases, stacked, preferred_element_type=jnp.float32)
    return bloch.reshape(2, kint.shape[0], Q, M, -1)


def rotate_modes(real_part, imag_part, vectors):
    er = vectors[:, 0]
    ei = vectors[:, 1]
    out_real = jnp.einsum("qvu,kqvx->kqux", er, real_part, precision=precise) - jnp.einsum(
        "qvu,kqvx->kqux", ei, imag_part, precision=precise
    )
    out_imag = jnp.einsum("qvu,kqvx->kqux", er, imag_part, precision=precise) + jnp.einsum(
        "qvu,kqvx->kqux", ei, real_part, precision=precise
    )
    return (out_real, out_imag)


def project_right(real_part, imag_part, factor):
    fr = factor[:, 0]
    fi = factor[:, 1]
    out_real = jnp.einsum("rmn,rnj->rmj", real_part, fr, precision=precise) - jnp.einsum(
        "rmn,rnj->rmj", imag_part, fi, precision=precise
    )
    out_imag = jnp.einsum("rmn,rnj->rmj", real_part, fi, precision=precise) + jnp.einsum(
        "rmn,rnj->rmj", imag_part, fr, precision=precise
    )
    return jnp.stack([out_real, out_imag], axis=1)


def project_left(values, factor):
    fr = factor[:, 0]
    fi = factor[:, 1]
    xr = values[:, 0]
    xi = values[:, 1]
    out_real = jnp.einsum("rmi,rmj->rij", fr, xr, precision=precise) + jnp.einsum(
        "rmi,rmj->rij", fi, xi, precision=precise
    )
    out_imag = jnp.einsum("rmi,rmj->rij", fr, xi, precision=precise) - jnp.einsum(
        "rmi,rmj->rij", fi, xr, precision=precise
    )
    return jnp.stack([out_real, out_imag], axis=1)


def plus_bands(plus_index, band_vectors, pair_ids):
    targets = plus_index[pair_ids // Q, pair_ids % Q]
    every_band = lax.all_gather(band_vectors, "kq", axis=0, tiled=True)
    return every_band[targets]


def shards(couplings, re_vectors, degeneracy, kpoints, plus_index, mode_vectors, band_vectors):
    local_count = kpoints.shape[0]
    local_rows = local_count * Q * M
    share_rows = local_rows // lax.axis_size("re")
    share_pairs = share_rows // M
    share_ids = lax.axis_index("re") * share_rows + jnp.arange(share_rows, dtype=jnp.int32)
    pair_share = lax.axis_index("re") * share_pairs + jnp.arange(share_pairs, dtype=jnp.int32)
    local_share = jnp.arange(share_rows, dtype=jnp.int32) // M
    moved = lax.all_to_all(couplings, "re", split_axis=4, concat_axis=1, tiled=True)
    lattice_all, degen_all = (
        lax.all_gather(re_vectors, "re", axis=0, tiled=True),
        lax.all_gather(degeneracy, "re", axis=0, tiled=True),
    )
    columns = moved.shape[4]
    bloch = phase_sum(kpoints, lattice_all, degen_all, moved)
    moded_real, moded_imag = rotate_modes(bloch[0], bloch[1], mode_vectors)
    paired = jnp.stack([moded_real, moded_imag]).reshape(2, local_rows, columns)
    returned = lax.all_to_all(paired, "re", split_axis=1, concat_axis=2, tiled=True)
    right = project_right(
        returned[0].reshape(share_rows, W, W),
        returned[1].reshape(share_rows, W, W),
        band_vectors[share_ids // (Q * M)],
    )
    fetched = plus_bands(plus_index, band_vectors, pair_share)
    result = project_left(right, fetched[local_share])
    return result.reshape(1, 1, share_rows, 2 * NB * NB)


MESH = pl.DeviceIdType.MESH
LANES = 640
GEO = 576
f32 = jnp.float32
bf16 = jnp.bfloat16
NT = (((1,), (1,)), ((), ()))
TN = (((0,), (0,)), ((), ()))


def iota(shape, axis):
    return lax.broadcasted_iota(jnp.int32, shape, axis)


def exact(a, b, dims=(((1,), (0,)), ((), ()))):
    return lax.dot_general(a, b, dims, precision=precise, preferred_element_type=f32)


def split(a):
    high = a.astype(bf16)
    return high, (a - high.astype(f32)).astype(bf16)


def dot16(a, b):
    return jnp.dot(a, b, preferred_element_type=f32)


def unit_cosine(step):
    step = step - NG * jnp.floor(step * (1.0 / NG))
    fold = jnp.minimum(step, NG - step)
    near = jnp.minimum(fold, 8.0 - fold)
    size = jnp.where(near < 0.5, 1.0, jnp.where(near < 1.5, math.cos(math.pi / 8), math.cos(math.pi / 4)))
    size = jnp.where(near > 2.5, math.cos(3 * math.pi / 8), size)
    size = jnp.where(near > 3.5, 0.0, size)
    return jnp.where(fold > 4.5, -size, size)


def quarter_swap(parts):
    lane = iota(parts[0].shape, 1)
    upper = (lane & 64) != 0
    odd = (lane & 32) != 0
    stage = list(parts)
    for a, b in ((0, 2), (1, 3)):
        moved = pltpu.roll(jnp.where(upper, parts[a], parts[b]), 64, 1)
        stage[a] = jnp.where(upper, moved, parts[a])
        stage[b] = jnp.where(upper, parts[b], moved)
    out = list(stage)
    for a, b in ((0, 1), (2, 3)):
        out[a] = jnp.where(odd, pltpu.roll(stage[b], 32, 1), stage[a])
        out[b] = jnp.where(odd, stage[b], pltpu.roll(stage[a], 96, 1))
    return out


def group_swap(x):
    sub = iota(x.shape, 0)
    group = iota(x.shape, 1) // 16
    rows = x.shape[0]
    for s in (4, 2, 1):
        low_a = (sub & s) == 0
        low_b = (group & s) == 0
        down = pltpu.roll(pltpu.roll(x, rows - s, 0), 16 * s, 1)
        up = pltpu.roll(pltpu.roll(x, s, 0), 128 - 16 * s, 1)
        x = jnp.where(low_a == low_b, x, jnp.where(low_a, down, up))
    return x


def unpack_bands(tile):
    return jnp.concatenate([tile] + [pltpu.roll(tile, 128 - 32 * g, 1) for g in (1, 2, 3)], axis=0)


def kernel(
    n_re, n_kq, coup_any, rvec_any, degen_any, kp_any, plus_any, mode_any, bands_any, out,
    coup, rvec, degen_own, kp_own, plus, mode, bands,
    F, Y, X, S, D, BZ, KP, bz, kp, fetch, send1, recv1, send2, recv2, sendb, recvb,
):
    re = lax.axis_index("re")
    kq = lax.axis_index("kq")
    n_all = n_re * n_kq
    me = kq * n_re + re
    width = n_re * W
    tiles = width // 128
    mine = pl.ds(pl.multiple_of(kq * width, width), width)
    pairs = [
        (coup_any.at[:, :, :, :, mine], coup),
        (rvec_any, rvec),
        (degen_any, degen_own),
        (kp_any, kp_own),
        (bands_any, bands),
        (plus_any, plus),
        (mode_any, mode),
    ]
    loads = [pltpu.make_async_copy(a, b, fetch.at[n]) for n, (a, b) in enumerate(pairs)]
    for load in loads:
        load.start()
    barrier = pltpu.get_barrier_semaphore()

    for off in range(1, n_all):
        to = lax.rem(me + off, n_all)
        pl.semaphore_signal(
            barrier, inc=1, device_id=(lax.rem(to, n_re), to // n_re), device_id_type=MESH
        )

    for n in range(4):
        loads[n].wait()
    kp[...] = jnp.zeros_like(kp)
    kp[0:3, 0 : kp_own.shape[1]] = kp_own[...].astype(f32)
    row = iota((16, 128), 0) // 2 % 4
    lane = iota((16, 128), 1)
    spare = jnp.zeros((16, 128), f32)
    for r in range(4):
        for d in range(4):
            value = (rvec[r, d] if d < 3 else degen_own[r]).astype(f32)
            spare = jnp.where((row == r) & (lane == 64 + d), value, spare)
    for t in range(tiles):
        for a in range(8):
            F[t, :, 2 * a : 2 * a + 2, :] = coup[a // 4, a % 4, :, :, t * 128 : t * 128 + 128].astype(f32)
        for v4 in range(5):
            parts = []
            for v in range(4 * v4, 4 * v4 + 4):
                parts.append(F[t, v] if v < M else jnp.zeros((16, 128), f32))
            moved = quarter_swap(parts)
            for m in range(4):
                piece = moved[m] + spare if v4 == 4 else moved[m]
                Y[t * 4 + m, :, v4 * 128 : v4 * 128 + 128] = piece.astype(bf16)

    pl.semaphore_wait(barrier, n_all - 1)

    def first(to, frm):
        return pltpu.make_async_remote_copy(
            src_ref=Y.at[to], dst_ref=X.at[frm],
            send_sem=send1, recv_sem=recv1,
            device_id=(to, kq), device_id_type=MESH,
        )

    def swap(ref, full, s, off):
        other = lax.rem(kq + off, n_kq)
        return pltpu.make_async_remote_copy(
            src_ref=ref, dst_ref=full.at[kq],
            send_sem=sendb.at[s, other], recv_sem=recvb.at[s, kq],
            device_id=(re, other), device_id_type=MESH,
        )

    def swapped(ref, full, s, off):
        other = lax.rem(kq + off, n_kq)
        return pltpu.make_async_remote_copy(
            src_ref=ref, dst_ref=full.at[other],
            send_sem=sendb.at[s, other], recv_sem=recvb.at[s, other],
            device_id=(re, other), device_id_type=MESH,
        )

    for off in range(1, n_kq):
        swap(kp, KP, 0, off).start()

    for off in range(1, n_re):
        first(lax.rem(re + off, n_re), re).start()
    loads[4].wait()
    for g in range(4):
        bz[:, :, g * 32 : g * 32 + 32] = bands[:, g // 2, g % 2 * 8 : g % 2 * 8 + 8, :]
    for off in range(1, n_kq):
        swap(bz, BZ, 1, off).start()
    loads[5].wait()
    loads[6].wait()
    X[re] = Y[re]
    KP[kq] = kp[...]
    BZ[kq] = bz[...]
    for off in range(1, n_kq):
        swapped(kp, KP, 0, off).wait_recv()
    n_dev = bz.shape[0]
    rows = n_kq * n_dev * 4
    points = KP[0]
    for other in range(1, n_kq):
        points = points + pltpu.roll(KP[other], other * n_dev, 1)
    points = jnp.concatenate([jnp.zeros((64, 128), f32), points, jnp.zeros((56, 128), f32)], axis=0)
    pick = ((iota((rows, 128), 0) // 4) == iota((rows, 128), 1)).astype(bf16)
    grid = lax.dot_general(pick, points.astype(bf16), NT, preferred_element_type=f32).astype(bf16)

    every1 = pltpu.make_async_remote_copy(
        src_ref=Y.at[0 : n_re - 1], dst_ref=X.at[0 : n_re - 1], send_sem=send1, recv_sem=recv1,
        device_id=(lax.rem(re + 1, n_re), kq), device_id_type=MESH,
    )
    every1.wait_recv()
    depth = n_re * 16
    lattice = X[:, :, 512:640].reshape(depth, 128)
    product = lax.dot_general(grid, lattice, NT, preferred_element_type=f32)
    ones = (iota((rows, 128), 1) == 67).astype(bf16)
    degen = lax.dot_general(ones, lattice, NT, preferred_element_type=f32)
    row = iota((rows, depth), 0)
    col = iota((rows, depth), 1)
    turn = (((col // 8) & 1) - (row & 1)).astype(f32) * 4.0
    same = ((row // 2) & 1) == (col & 1)
    phases = jnp.where(same, unit_cosine(product + turn) * (1.0 / degen), 0.0).astype(bf16)
    for t in range(5):
        lanes = slice(t * 128, t * 128 + 128)
        bloch = dot16(phases, X[:, :, lanes].reshape(depth, 128))
        S[:, :, lanes] = bloch.reshape(n_all, 8, 128).astype(bf16)

    def second(to, frm):
        return pltpu.make_async_remote_copy(
            src_ref=S.at[to], dst_ref=D.at[frm],
            send_sem=send2, recv_sem=recv2,
            device_id=(lax.rem(to, n_re), to // n_re), device_id_type=MESH,
        )

    offsets = list(range(n_re - 1, 0, -1))
    for off in offsets + [0]:
        for turn in range(n_kq):
            if off or turn:
                to = lax.rem(kq + turn, n_kq) * n_re + jnp.bitwise_xor(re, off)
                second(to, me).start()
    D[me] = S[me]

    for off in range(1, n_kq):
        swapped(bz, BZ, 1, off).wait_recv()
    spread = (iota((128, 256), 0) == iota((128, 256), 1) // 8).astype(f32)
    lane = iota((NB, 256), 1)
    imag_in = (lane & 1) == 1
    left = []
    for p in range(4):
        target = plus[p % 2, re * 2 + p // 2]
        tile = BZ[target // n_dev, lax.rem(target, n_dev)]
        wide = exact(unpack_bands(tile), spread)
        real, imag = wide[:NB], wide[NB:]
        own = ((lane // 2) & 3) == p
        left.append(jnp.where(own, jnp.where(imag_in, imag, real), 0.0))
        left.append(jnp.where(own, jnp.where(imag_in, real, -imag), 0.0))
    left_high, left_low = split(jnp.concatenate(left, axis=0))
    left_both = jnp.concatenate([left_high, left_low], axis=0)
    down = ((iota((256, 128), 0) & 31) == iota((256, 128), 1)).astype(f32)
    lane = iota((32, 256), 1)
    across = iota((32, 256), 0) == (lane // 128) * NB + (lane & 15)
    flip = iota((32, 256), 0) == (1 - lane // 128) * NB + (lane & 15)
    minus = jnp.where(lane < 128, -1.0, 1.0)
    same_mode = iota((256, 256), 0) // 32 == (iota((256, 256), 1) // NB) % 8
    right = []
    for k in range(2):
        tall = exact(down, unpack_bands(bz[re * 2 + k]), NT)
        a = exact(tall, across.astype(f32))
        b = exact(tall, jnp.where(flip, minus, 0.0))
        right.append([split(jnp.where(same_mode, w, 0.0)) for w in (a, b)])

    every2 = pltpu.make_async_remote_copy(
        src_ref=S.at[0 : n_all - 1], dst_ref=D.at[0 : n_all - 1], send_sem=send2, recv_sem=recv2,
        device_id=(lax.rem(re + 1, n_re), kq), device_id_type=MESH,
    )
    every2.wait_recv()
    data = D[...].astype(f32).reshape(n_all * 8, LANES).astype(bf16)
    both = dot16(left_both, data)
    summed = both[:128] + both[128:]
    groups = [
        summed[:, 0:256],
        summed[:, 256:512],
        jnp.concatenate([summed[:, 512:640], jnp.zeros((128, 128), f32)], axis=1),
    ]
    values = [[None, None], [None, None]]
    for k in range(2):
        total = None
        for c in range(2):
            x = jnp.concatenate(
                [g[((k * 2 + q) * 2 + c) * NB : ((k * 2 + q) * 2 + c + 1) * NB] for g in groups for q in range(2)],
                axis=0,
            )
            high, low = split(x)
            w_high, w_low = right[k][c]
            term = dot16(high, w_high) + dot16(low, w_high) + dot16(high, w_low)
            total = term if total is None else total + term
        for c in range(2):
            turned = group_swap(total[:, c * 128 : c * 128 + 128])
            for q in range(2):
                values[q][c] = (values[q][c] or []) + [
                    jnp.concatenate(
                        [
                            jnp.concatenate(
                                [turned[(g * 2 + q) * NB + h * 8 : (g * 2 + q) * NB + h * 8 + 8] for g in range(3)],
                                axis=0,
                            )
                            for h in range(2)
                        ],
                        axis=1,
                    )
                ]
    for q in range(2):
        xr = jnp.concatenate(values[q][0], axis=1)[:M]
        xi = jnp.concatenate(values[q][1], axis=1)[:M]
        er, ei = mode[q, :, 0, :], mode[q, :, 1, :]
        yr = exact(er, xr, TN) - exact(ei, xi, TN)
        yi = exact(er, xi, TN) + exact(ei, xr, TN)
        for k in range(2):
            at = (k * 2 + q) * M
            out[0, 0, at : at + M, 0:256] = yr[:, k * 256 : k * 256 + 256]
            out[0, 0, at : at + M, 256:512] = yi[:, k * 256 : k * 256 + 256]

    for off in range(1, n_kq):
        swap(kp, KP, 0, off).wait_send()
        swap(bz, BZ, 1, off).wait_send()

    every1.wait_send()
    every2.wait_send()


def fused(n_re, n_kq, couplings, re_vectors, degeneracy, kpoints, plus_index, mode_vectors, band_vectors):
    n_all = n_re * n_kq
    k_dev = kpoints.shape[0]
    vmem = pl.BlockSpec(memory_space=pltpu.VMEM)
    return pl.pallas_call(
        functools.partial(kernel, n_re, n_kq),
        out_shape=jax.ShapeDtypeStruct((1, 1, k_dev * Q * M // n_re, 2 * NB * NB), f32),
        in_specs=[pl.BlockSpec(memory_space=pltpu.HBM)] * 7,
        out_specs=vmem,
        scratch_shapes=[
            pltpu.VMEM((2, 4, M, Q, n_re * W), bf16),
            pltpu.SMEM((4, 3), jnp.int32),
            pltpu.SMEM((4,), jnp.int32),
            pltpu.VMEM((3, k_dev), jnp.int32),
            pltpu.SMEM((Q, k_dev), jnp.int32),
            pltpu.VMEM((Q, M, 2, M), f32),
            pltpu.VMEM((k_dev, 2, NB, W), f32),
            pltpu.VMEM((n_re * W // 128, M, 16, 128), f32),
            pltpu.VMEM((n_re, 16, LANES), bf16),
            pltpu.VMEM((n_re, 16, LANES), bf16),
            pltpu.VMEM((n_all, 8, LANES), bf16),
            pltpu.VMEM((n_all, 8, LANES), bf16),
            pltpu.VMEM((n_kq, k_dev, 8, 128), f32),
            pltpu.VMEM((n_kq, 8, 128), f32),
            pltpu.VMEM((k_dev, 8, 128), f32),
            pltpu.VMEM((8, 128), f32),
            pltpu.SemaphoreType.DMA((7,)),
            pltpu.SemaphoreType.DMA,
            pltpu.SemaphoreType.DMA,
            pltpu.SemaphoreType.DMA,
            pltpu.SemaphoreType.DMA,
            pltpu.SemaphoreType.DMA((2, n_kq)),
            pltpu.SemaphoreType.DMA((2, n_kq)),
        ],
        compiler_params=pltpu.CompilerParams(
            collective_id=0, has_side_effects=True, vmem_limit_bytes=60 * 1024 * 1024
        ),
    )(
        couplings.transpose(0, 1, 3, 2, 4),
        re_vectors,
        degeneracy,
        kpoints.T,
        plus_index.T,
        mode_vectors.transpose(0, 2, 1, 3),
        band_vectors.transpose(0, 1, 3, 2),
    )


def solution(mesh):
    n_re, n_kq = mesh.shape["re"], mesh.shape["kq"]
    body = functools.partial(fused, n_re, n_kq) if (n_re, n_kq) == (NB, W // NB) else shards
    return jax.shard_map(
        body,
        mesh=mesh,
        in_specs=(
            P(None, "re", None, None, None),
            P("re", None),
            P("re"),
            P("kq", None),
            P("kq", None),
            P(),
            P("kq", None, None, None),
        ),
        out_specs=P("kq", "re", None, None),
        check_vma=False,
    )
```
